128 devices in a mesh: view: 2 (over z_lo), dp: 64 (over y, z_hi, x, core).
Axes of the slice: x: 4, y: 4, z: 4 (z_hi: 2, z_lo: 2; z = z_hi * 2 + z_lo), core: 2. Of those that a mesh axis runs over, the one named last changes fastest.
Arguments:
- hidden: bfloat16 [2, 896, 4096], P('view', 'dp')
- weight: bfloat16 [4096, 8192], P(None, 'dp')
Outputs:
- grad_hidden: float32 [2, 896, 4096], P('view', 'dp')
- grad_weight: float32 [4096, 8192], P(None, 'dp')
All inputs are finite; a program needn't handle non-finite values.
Results may differ from the reference program's by a relative error of at most 0.003.
Values may be sent and summed in bfloat16 or wider, within the bound.
No kernel may reach another device: no remote copies, remote signals or barrier semaphores. Data moves between devices by JAX's collectives and lax.ppermute only.
A program may use at most 128 MiB of HBM per device.

```python
import math
import jax
import jax.numpy as jnp
from jax import lax

IN_UNITS = 4096
OUT_UNITS = 8192
VIEW_BATCH = 896


def draw_hidden(key, part):
    keys = jax.random.split(jax.random.fold_in(key, 7), 4)
    shared = jax.random.normal(keys[0], (VIEW_BATCH, IN_UNITS), jnp.float32)
    own_noise = jax.random.normal(keys[1], (2, VIEW_BATCH, IN_UNITS), jnp.float32)
    low_end = math.log(0.5)
    high_end = math.log(2.0)
    column_scale = jnp.exp(jax.random.uniform(keys[2], (IN_UNITS,), jnp.float32, low_end, high_end))
    sample_scale = jnp.exp(jax.random.uniform(keys[3], (2, VIEW_BATCH, 1), jnp.float32, math.log(0.5), math.log(2.0)))
    before = shared[None] + 0.6 * own_noise
    return (jnp.maximum(before, 0.0) * column_scale * sample_scale).astype(jnp.bfloat16)


def draw_weight(key, part):
    keys = jax.random.split(jax.random.fold_in(key, 13), 2)
    entries = jax.random.normal(keys[0], (IN_UNITS, OUT_UNITS), jnp.float32)
    column_scale = jnp.exp(jax.random.uniform(keys[1], (OUT_UNITS,), jnp.float32, math.log(0.5), math.log(2.0)))
    return (entries * column_scale / math.sqrt(IN_UNITS)).astype(jnp.bfloat16)


def setup_inputs(seed: int = 0) -> dict:
    splits = jax.random.split(jax.random.key(seed), 3)
    hidden = draw_hidden(jax.random.fold_in(splits[2], 71), 0)
    weight = draw_weight(jax.random.fold_in(splits[2], 71), 0)
    return {"hidden": hidden, "weight": weight}


def view_gradient(embedded, partner):
    total_rows = embedded.shape[0]
    embed_wide = embedded.astype(jnp.float32)
    centered = (embed_wide - lax.optimization_barrier(jnp.mean(embed_wide, axis=0, keepdims=True))).astype(jnp.bfloat16)
    centered_wide = centered.astype(jnp.float32)
    sum_squares = lax.optimization_barrier(jnp.sum(centered_wide * centered_wide, axis=0, keepdims=True))
    spread_std = jnp.sqrt(sum_squares / (total_rows - 1) + 0.0001)
    sample_gram = jnp.dot(centered_wide, centered_wide.T, precision=lax.Precision.HIGHEST)
    coupled = jnp.dot(sample_gram, centered_wide, precision=lax.Precision.HIGHEST)
    coef_var = total_rows / (2.0 * (total_rows - 1))
    coef_cov = 0.08 * total_rows / ((total_rows - 1) * (total_rows - 1))
    hinge_weight = jax.nn.sigmoid(10.0 * (1.0 - spread_std))
    result = embed_wide - partner.astype(jnp.float32) - coef_var * hinge_weight * centered_wide / spread_std
    result = result + coef_cov * (coupled - centered_wide * sum_squares)
    return result.astype(jnp.bfloat16)

def reference(hidden, weight):
    first = jnp.dot(hidden[0], weight, preferred_element_type=jnp.float32).astype(jnp.bfloat16)
    second = jnp.dot(hidden[1], weight, preferred_element_type=jnp.float32).astype(jnp.bfloat16)
    grad_first = view_gradient(first, second)
    grad_second = view_gradient(second, first)
    hidden_first = jnp.dot(grad_first, weight.T, preferred_element_type=jnp.float32)
    hidden_second = jnp.dot(grad_second, weight.T, preferred_element_type=jnp.float32)
    weight_total = jnp.dot(hidden[0].T, grad_first, preferred_element_type=jnp.float32)
    weight_total = weight_total + jnp.dot(hidden[1].T, grad_second, preferred_element_type=jnp.float32)
    grad_weight = weight_total / jnp.sqrt(2.0 * hidden.shape[1])
    return (jnp.stack([hidden_first, hidden_second]), grad_weight)
```

```python
import jax
import jax.numpy as jnp
from jax import lax
from jax.sharding import PartitionSpec as P

YS, ZS, XS, CS = 4, 2, 4, 2
DP = YS * ZS * XS * CS
PAD = 16


def place(d):
    return (d // (ZS * XS * CS), d // (XS * CS) % ZS, d // CS % XS, d % CS)


def index(y, z, x, c):
    return ((y * ZS + z) * XS + x) * CS + c


def groups(axes):
    found = {}
    for d in range(DP):
        key = tuple(p for p, name in zip(place(d), "yzxc") if name not in axes)
        found.setdefault(key, []).append(d)
    return list(found.values())


def swap(block, view=0, z=0, c=0):
    route = []
    for v in range(2):
        for d in range(DP):
            y, zd, x, cd = place(d)
            route.append((v * DP + d, (v ^ view) * DP + index(y, zd ^ z, x, cd ^ c)))
    return lax.ppermute(block, ("view", "dp"), route)


def exchange(blocks, axes):
    return lax.all_to_all(blocks, "dp", 0, 0, tiled=True, axis_index_groups=groups(axes))


def matmul(a, b, a_dim, b_dim):
    return lax.dot_general(
        a, b, (((a_dim,), (b_dim,)), ((), ())), preferred_element_type=jnp.float32
    )


def rounded(values):
    return lax.optimization_barrier(values.astype(jnp.bfloat16))


def flip(block):
    n = block.shape[1] // 128
    runs = [block[:, 128 * (i ^ 1) : 128 * (i ^ 1) + 128] for i in range(n)]
    return jnp.concatenate(runs, axis=1)


def ordered(first, second, swapped):
    return jnp.where(
        swapped,
        jnp.concatenate([second, first], axis=0),
        jnp.concatenate([first, second], axis=0),
    )


def on_device(hidden, weight):
    rows = hidden.shape[1]
    samples = rows * DP
    half = hidden.shape[2] // 2
    units = weight.shape[1]
    d = lax.axis_index("dp")
    core = d % CS
    z = d // (XS * CS) % ZS

    w_own = lax.dynamic_slice(weight, (core * half, 0), (half, units))
    w_give = lax.dynamic_slice(weight, ((1 - core) * half, 0), (half, units))
    w_far = swap(w_own, view=1, z=1)
    w_far_sib = swap(w_give, view=1, z=1, c=1)
    w_sib = swap(w_give, c=1)

    padded = jnp.pad(hidden[0], ((0, PAD - rows), (0, 0)))
    halves = padded.reshape(PAD, 2, half).transpose(1, 0, 2)
    copies = jnp.broadcast_to(halves[None], (YS * XS, 2, PAD, half))
    plane = exchange(copies.reshape(YS * XS * 2 * PAD, half), "yxc")
    other_plane = swap(plane, z=1)
    span = plane.shape[0]

    w_all = jnp.concatenate([w_own, w_sib, w_far, w_far_sib], axis=1)
    part = matmul(plane, w_all, 1, 0)
    embedded = rounded(part + flip(swap(part, c=1)))
    chip = 2 * units
    from_other = swap(embedded[:, chip:], z=1)
    embedded = ordered(embedded[:, :chip], from_other, z == 1)

    wide = embedded.astype(jnp.float32)
    real = (lax.broadcasted_iota(jnp.int32, (2 * span, 1), 0) % PAD) < rows
    mean = jnp.sum(wide, axis=0, keepdims=True) / samples
    centered = rounded(jnp.where(real, wide - mean, 0.0))
    centered_wide = centered.astype(jnp.float32)
    sum_squares = jnp.sum(centered_wide * centered_wide, axis=0, keepdims=True)
    spread_std = jnp.sqrt(sum_squares / (samples - 1) + 0.0001)

    embedded_half = lax.dynamic_slice(embedded, (core * span, 0), (span, chip))
    partner = swap(embedded_half, view=1)
    centered_half = lax.dynamic_slice(centered, (core * span, 0), (span, chip))

    gram = matmul(centered_half, centered, 1, 1).astype(jnp.bfloat16)
    gram = exchange(gram, "yzx").reshape(YS * ZS * XS, PAD, 2 * span)
    gram = jnp.sum(gram.astype(jnp.float32), axis=0).astype(jnp.bfloat16)
    gram = jnp.broadcast_to(gram[None], (YS * ZS * XS, PAD, 2 * span))
    gram = exchange(gram.reshape(span, 2 * span), "yzx")
    coupled = matmul(gram, centered, 1, 0)

    coef_var = samples / (2.0 * (samples - 1))
    coef_cov = 0.08 * samples / ((samples - 1) * (samples - 1))
    hinge = jax.nn.sigmoid(10.0 * (1.0 - spread_std))
    wide_half = centered_half.astype(jnp.float32)
    combined = (
        embedded_half.astype(jnp.float32)
        - partner.astype(jnp.float32)
        - coef_var * hinge * wide_half / spread_std
        + coef_cov * (coupled - wide_half * sum_squares)
    )
    grad = rounded(combined)
    grad = ordered(grad, flip(swap(grad, c=1)), core == 1)
    grad_plane = lax.dynamic_slice(grad, (z * span, 0), (span, chip))
    grad_other = lax.dynamic_slice(grad, ((1 - z) * span, 0), (span, chip))
    grad_far = swap(grad_other, z=1)

    w_part = rounded(matmul(plane, grad_plane, 0, 0) + matmul(other_plane, grad_other, 0, 0))
    mine = w_part[:, :units]
    theirs = w_part[:, units:]
    mine_view = swap(mine, view=1)
    sib_view = swap(theirs, view=1, c=1)
    sib = swap(theirs, c=1)

    grad_all = jnp.concatenate([grad_plane, grad_far], axis=1)
    h_part = matmul(grad_all, w_all, 1, 1).astype(jnp.bfloat16)
    pieces = exchange(h_part, "yxc").reshape(YS * XS, 2, PAD, half)
    total = jnp.sum(pieces.astype(jnp.float32), axis=0)
    grad_rows = total.transpose(1, 0, 2).reshape(PAD, 2 * half)[:rows]

    wide_sum = lambda a, b: a.astype(jnp.float32) + b.astype(jnp.float32)
    grad_weight = ordered(wide_sum(mine, mine_view), wide_sum(sib, sib_view), core == 1)
    return (grad_rows[None], grad_weight / jnp.sqrt(2.0 * samples))


def solution(mesh):
    return jax.shard_map(
        on_device,
        mesh=mesh,
        in_specs=(P("view", "dp", None), P(None, "dp")),
        out_specs=(P("view", "dp", None), P(None, "dp")),
        check_vma=False,
    )
```

```python
import jax
import jax.numpy as jnp
from jax import lax
from jax.sharding import PartitionSpec as P

YS, ZS, XS, CS = 4, 2, 4, 2
DP = YS * ZS * XS * CS
PAD = 16


def place(d):
    return (d // (ZS * XS * CS), d // (XS * CS) % ZS, d // CS % XS, d % CS)


def index(y, z, x, c):
    return ((y * ZS + z) * XS + x) * CS + c


def groups(axes):
    found = {}
    for d in range(DP):
        key = tuple(p for p, name in zip(place(d), "yzxc") if name not in axes)
        found.setdefault(key, []).append(d)
    return list(found.values())


def swap(block, view=0, z=0, c=0):
    route = []
    for v in range(2):
        for d in range(DP):
            y, zd, x, cd = place(d)
            route.append((v * DP + d, (v ^ view) * DP + index(y, zd ^ z, x, cd ^ c)))
    return lax.ppermute(block, ("view", "dp"), route)


def exchange(blocks, axes):
    return lax.all_to_all(blocks, "dp", 0, 0, tiled=True, axis_index_groups=groups(axes))


def matmul(a, b, a_dim, b_dim):
    return lax.dot_general(
        a, b, (((a_dim,), (b_dim,)), ((), ())), preferred_element_type=jnp.float32
    )


def rounded(values):
    return lax.optimization_barrier(values.astype(jnp.bfloat16))


def flip(block):
    n = block.shape[1] // 2
    return jnp.concatenate([block[:, n:], block[:, :n]], axis=1)


def ordered(first, second, swapped):
    return jnp.where(
        swapped,
        jnp.concatenate([second, first], axis=0),
        jnp.concatenate([first, second], axis=0),
    )


def wide_sum(a, b):
    return a.astype(jnp.float32) + b.astype(jnp.float32)


def on_device(hidden, weight):
    rows = hidden.shape[1]
    samples = rows * DP
    half = hidden.shape[2] // 2
    units = weight.shape[1]
    d = lax.axis_index("dp")
    core = d % CS
    z = d // (XS * CS) % ZS

    w_own = lax.dynamic_slice(weight, (core * half, 0), (half, units))
    w_give = lax.dynamic_slice(weight, ((1 - core) * half, 0), (half, units))
    w_far = swap(w_own, view=1, z=1)
    w_far_sib = swap(w_give, view=1, z=1, c=1)
    w_sib = swap(w_give, c=1)

    padded = jnp.pad(hidden[0], ((0, PAD - rows), (0, 0)))
    halves = padded.reshape(PAD, 2, half).transpose(1, 0, 2)
    copies = jnp.broadcast_to(halves[None], (YS * XS, 2, PAD, half))
    plane = exchange(copies.reshape(YS * XS * 2 * PAD, half), "yxc")
    span = plane.shape[0]
    pair = 2 * units

    w_all = jnp.concatenate([w_own, w_far, w_sib, w_far_sib], axis=1)
    part = matmul(plane, w_all, 1, 0)
    embedded = rounded(part[:, :pair] + swap(part[:, pair:], c=1))
    from_other = swap(embedded, z=1)
    embedded = ordered(embedded, flip(from_other), z == 1)
    embedded = jnp.concatenate([embedded, swap(embedded, c=1)], axis=1)

    cuts = ((0, 896), (896, 1536), (1536, half))
    plane_late, _ = lax.optimization_barrier((plane, from_other))
    others = [swap(plane_late[:, low:high], z=1) for low, high in cuts]

    wide = embedded.astype(jnp.float32)
    real = (lax.broadcasted_iota(jnp.int32, (2 * span, 1), 0) % PAD) < rows
    mean = jnp.sum(wide, axis=0, keepdims=True) / samples
    centered = rounded(jnp.where(real, wide - mean, 0.0))
    centered_wide = centered.astype(jnp.float32)
    sum_squares = jnp.sum(centered_wide * centered_wide, axis=0, keepdims=True)
    spread_std = jnp.sqrt(sum_squares / (samples - 1) + 0.0001)

    quarter = span // 2
    at = (z * 2 + core) * quarter
    embedded_part = lax.dynamic_slice(embedded, (at, 0), (quarter, 2 * pair))
    partner = swap(embedded_part, view=1)
    centered_part = lax.dynamic_slice(centered, (at, 0), (quarter, 2 * pair))

    peers = YS * XS
    gram = matmul(centered_part, centered, 1, 1).astype(jnp.bfloat16)
    gram = exchange(gram, "yx").reshape(peers, PAD, 2 * span)
    gram = jnp.sum(gram.astype(jnp.float32), axis=0).astype(jnp.bfloat16)
    gram, others[0] = lax.optimization_barrier((gram, others[0]))
    gram = jnp.broadcast_to(gram[None], (peers, PAD, 2 * span))
    gram = exchange(gram.reshape(quarter, 2 * span), "yx")
    gram, others[1] = lax.optimization_barrier((gram, others[1]))
    coupled = matmul(gram, centered, 1, 0)

    coef_var = samples / (2.0 * (samples - 1))
    coef_cov = 0.08 * samples / ((samples - 1) * (samples - 1))
    hinge = jax.nn.sigmoid(10.0 * (1.0 - spread_std))
    wide_part = centered_part.astype(jnp.float32)
    combined = (
        embedded_part.astype(jnp.float32)
        - partner.astype(jnp.float32)
        - coef_var * hinge * wide_part / spread_std
        + coef_cov * (coupled - wide_part * sum_squares)
    )
    grad = rounded(combined)
    grad_plane = ordered(grad, flip(swap(grad, c=1)), core == 1)
    far = jnp.concatenate([grad_plane[:, units:pair], grad_plane[:, pair + units :]], axis=1)
    near = jnp.concatenate([grad_plane[:, :units], grad_plane[:, pair : pair + units]], axis=1)
    grad_other = swap(far, z=1)

    h_part = matmul(grad_plane, w_all, 1, 1).astype(jnp.bfloat16)
    pieces = exchange(h_part, "yxc").reshape(peers, 2, PAD, half)
    total = jnp.sum(pieces.astype(jnp.float32), axis=0)
    grad_rows = total.transpose(1, 0, 2).reshape(PAD, 2 * half)[:rows]

    own_runs, sib_runs = [], []
    for low, high, parts in ((0, 896, others[:1]), (896, half, others[1:])):
        w_part = [matmul(part, grad_other, 0, 0) for part in parts]
        w_part = jnp.concatenate(w_part, axis=0) + matmul(plane[:, low:high], near, 0, 0)
        w_part = rounded(w_part)
        mine = w_part[:, :units]
        theirs = w_part[:, units:]
        own_runs.append(wide_sum(mine, swap(mine, view=1)))
        sib_runs.append(wide_sum(swap(theirs, c=1), swap(theirs, view=1, c=1)))
    grad_weight = ordered(
        jnp.concatenate(own_runs, axis=0), jnp.concatenate(sib_runs, axis=0), core == 1
    )
    return (grad_rows[None], grad_weight / jnp.sqrt(2.0 * samples))


def solution(mesh):
    return jax.shard_map(
        on_device,
        mesh=mesh,
        in_specs=(P("view", "dp", None), P(None, "dp")),
        out_specs=(P("view", "dp", None), P(None, "dp")),
        check_vma=False,
    )
```

```python
import jax
import jax.numpy as jnp
from jax import lax
from jax.sharding import PartitionSpec as P

YS, ZS, XS, CS = 4, 2, 4, 2
DP = YS * ZS * XS * CS
PAD = 16


def place(d):
    return (d // (ZS * XS * CS), d // (XS * CS) % ZS, d // CS % XS, d % CS)


def index(y, z, x, c):
    return ((y * ZS + z) * XS + x) * CS + c


def groups(axes):
    found = {}
    for d in range(DP):
        key = tuple(p for p, name in zip(place(d), "yzxc") if name not in axes)
        found.setdefault(key, []).append(d)
    return list(found.values())


def swap(block, view=0, z=0, c=0):
    route = []
    for v in range(2):
        for d in range(DP):
            y, zd, x, cd = place(d)
            route.append((v * DP + d, (v ^ view) * DP + index(y, zd ^ z, x, cd ^ c)))
    return lax.ppermute(block, ("view", "dp"), route)


def exchange(blocks, axes):
    return lax.all_to_all(blocks, "dp", 0, 0, tiled=True, axis_index_groups=groups(axes))


def matmul(a, b, a_dim, b_dim):
    return lax.dot_general(
        a, b, (((a_dim,), (b_dim,)), ((), ())), preferred_element_type=jnp.float32
    )


def rounded(values):
    return lax.optimization_barrier(values.astype(jnp.bfloat16))


def reordered(block, order):
    return jnp.concatenate([block[:, 128 * i : 128 * i + 128] for i in order], axis=1)


def wide_sum(a, b):
    return a.astype(jnp.float32) + b.astype(jnp.float32)


def on_device(hidden, weight):
    rows = hidden.shape[1]
    width = hidden.shape[2]
    samples = rows * DP
    units = weight.shape[1]
    peers = YS * XS

    w_far = swap(weight, view=1, z=1)
    w_sib = swap(weight, c=1)
    w_far_sib = swap(w_far, c=1)

    padded = jnp.pad(hidden[0], ((0, PAD - rows), (0, 0)))
    copies = jnp.broadcast_to(padded[None], (peers, PAD, width))
    plane = exchange(copies.reshape(peers * PAD, width), "yx")
    quarter = plane.shape[0]

    part = [matmul(plane, w, 1, 0) for w in (weight, w_sib, w_far, w_far_sib)]
    mine = rounded(jnp.concatenate(part, axis=1))
    from_sib = swap(mine, c=1)
    from_far = swap(mine, z=1)
    from_far_sib = swap(from_far, c=1)
    partner = swap(mine, view=1)
    embedded = jnp.concatenate(
        [
            mine,
            reordered(from_sib, (1, 0, 3, 2)),
            reordered(from_far, (2, 3, 0, 1)),
            reordered(from_far_sib, (3, 2, 1, 0)),
        ],
        axis=0,
    )

    cuts = ((0, 1792), (1792, 3072), (3072, width))
    plane_late, _ = lax.optimization_barrier((plane, from_far))
    h_sib = swap(plane, c=1)
    h_far = [swap(plane_late[:, low:high], z=1) for low, high in cuts]

    wide = embedded.astype(jnp.float32)
    real = (lax.broadcasted_iota(jnp.int32, (4 * quarter, 1), 0) % PAD) < rows
    mean = jnp.sum(wide, axis=0, keepdims=True) / samples
    centered = rounded(jnp.where(real, wide - mean, 0.0))
    centered_wide = centered.astype(jnp.float32)
    sum_squares = jnp.sum(centered_wide * centered_wide, axis=0, keepdims=True)
    spread_std = jnp.sqrt(sum_squares / (samples - 1) + 0.0001)

    gram = matmul(centered[:quarter], centered, 1, 1).astype(jnp.bfloat16)
    gram = exchange(gram, "yx").reshape(peers, PAD, 4 * quarter)
    gram = jnp.sum(gram.astype(jnp.float32), axis=0).astype(jnp.bfloat16)
    gram, h_far[0] = lax.optimization_barrier((gram, h_far[0]))
    gram = jnp.broadcast_to(gram[None], (peers, PAD, 4 * quarter))
    gram = exchange(gram.reshape(quarter, 4 * quarter), "yx")
    gram, h_far[1] = lax.optimization_barrier((gram, h_far[1]))
    coupled = matmul(gram, centered, 1, 0)

    coef_var = samples / (2.0 * (samples - 1))
    coef_cov = 0.08 * samples / ((samples - 1) * (samples - 1))
    hinge = jax.nn.sigmoid(10.0 * (1.0 - spread_std))
    centered_part = centered_wide[:quarter]
    combined = (
        mine.astype(jnp.float32)
        - partner.astype(jnp.float32)
        - coef_var * hinge * centered_part / spread_std
        + coef_cov * (coupled - centered_part * sum_squares)
    )
    grad = combined.astype(jnp.bfloat16)
    grad, h_far[2] = lax.optimization_barrier((grad, h_far[2]))
    run = lambda i: grad[:, units * i : units * i + units]
    g_far = swap(run(2), z=1)
    g_far_sib = swap(run(3), z=1, c=1)
    g_sib = swap(run(1), c=1)

    w_all = jnp.concatenate([weight, w_sib, w_far, w_far_sib], axis=1)
    h_part = matmul(grad, w_all, 1, 1).astype(jnp.bfloat16)
    pieces = exchange(h_part, "yx").reshape(peers, PAD, width)
    grad_rows = jnp.sum(pieces.astype(jnp.float32), axis=0)[:rows]

    runs = []
    for (low, high), far in zip(cuts, h_far):
        far_sib = swap(far, c=1)
        total = matmul(plane[:, low:high], run(0), 0, 0)
        total = total + matmul(h_sib[:, low:high], g_sib, 0, 0)
        total = total + matmul(far, g_far, 0, 0)
        total = rounded(total + matmul(far_sib, g_far_sib, 0, 0))
        runs.append(wide_sum(total, swap(total, view=1)))
    grad_weight = jnp.concatenate(runs, axis=0) / jnp.sqrt(2.0 * samples)
    return (grad_rows[None], grad_weight)


def solution(mesh):
    return jax.shard_map(
        on_device,
        mesh=mesh,
        in_specs=(P("view", "dp", None), P(None, "dp")),
        out_specs=(P("view", "dp", None), P(None, "dp")),
        check_vma=False,
    )
```

```python
import functools

import jax
import jax.numpy as jnp
from jax import lax
from jax.experimental import pallas as pl
from jax.experimental.pallas import tpu as pltpu
from jax.sharding import PartitionSpec as P

YS, ZS, XS, CS = 4, 2, 4, 2
DP = YS * ZS * XS * CS
PAD = 16
TILE = 512
VMEM = 40 * 1024 * 1024


def place(d):
    return (d // (ZS * XS * CS), d // (XS * CS) % ZS, d // CS % XS, d % CS)


def index(y, z, x, c):
    return ((y * ZS + z) * XS + x) * CS + c


def groups(axes):
    found = {}
    for d in range(DP):
        key = tuple(p for p, name in zip(place(d), "yzxc") if name not in axes)
        found.setdefault(key, []).append(d)
    return list(found.values())


def swap(block, view=0, z=0, c=0):
    route = []
    for v in range(2):
        for d in range(DP):
            y, zd, x, cd = place(d)
            route.append((v * DP + d, (v ^ view) * DP + index(y, zd ^ z, x, cd ^ c)))
    return lax.ppermute(block, ("view", "dp"), route)


def exchange(blocks, axes):
    return lax.all_to_all(blocks, "dp", 0, 0, tiled=True, axis_index_groups=groups(axes))


def matmul(a, b, a_dim, b_dim):
    return lax.dot_general(
        a, b, (((a_dim,), (b_dim,)), ((), ())), preferred_element_type=jnp.float32
    )


def reordered(block, order):
    return jnp.concatenate([block[:, 128 * i : 128 * i + 128] for i in order], axis=1)


def shape(dims, dtype=jnp.bfloat16):
    return jax.ShapeDtypeStruct(dims, dtype)


def params(steps=0):
    semantics = ("arbitrary",) * steps if steps else None
    return pltpu.CompilerParams(vmem_limit_bytes=VMEM, dimension_semantics=semantics)


def cost(flops, size):
    return pl.CostEstimate(flops=flops, bytes_accessed=size, transcendentals=0)


def without_padding(x, rows):
    n = x.shape[0] // PAD * rows
    out = lax.broadcasted_iota(jnp.int32, (n, x.shape[0]), 0)
    source = lax.broadcasted_iota(jnp.int32, (n, x.shape[0]), 1)
    pick = out + out // rows * (PAD - rows) == source
    return matmul(jnp.where(pick, 1.0, 0.0).astype(x.dtype), x, 1, 0).astype(x.dtype)


def compact_kernel(rows, x_ref, *o_refs):
    at = 0
    for ref in o_refs:
        n = ref.shape[1]
        ref[...] = without_padding(x_ref[:, at : at + n], rows)
        at += n


def compact(block, rows, widths):
    n = block.shape[0] // PAD * rows
    return pl.pallas_call(
        functools.partial(compact_kernel, rows),
        out_shape=tuple(shape((n, width)) for width in widths),
        compiler_params=params(),
        cost_estimate=cost(2 * n * block.size, 4 * block.size),
    )(block)


def copies_kernel(x_ref, o_ref):
    x = x_ref[0]
    zeros = jnp.zeros((PAD - x.shape[0], x.shape[1]), x.dtype)
    x = jnp.concatenate([x, zeros], axis=0)
    for i in range(o_ref.shape[0] // PAD):
        o_ref[PAD * i : PAD * i + PAD, :] = x


def embed_kernel(h_ref, a_ref, b_ref, c_ref, d_ref, o_ref, acc_ref):
    step = pl.program_id(0)

    @pl.when(step == 0)
    def _():
        acc_ref[...] = jnp.zeros_like(acc_ref)

    w = jnp.concatenate([a_ref[...], b_ref[...], c_ref[...], d_ref[...]], axis=1)
    acc_ref[...] += matmul(h_ref[...], w, 1, 0)

    @pl.when(step == pl.num_programs(0) - 1)
    def _():
        o_ref[...] = acc_ref[...].astype(o_ref.dtype)


def center_kernel(rows, samples, own_ref, sib_ref, far_ref, far_sib_ref, c_ref, f_ref, g_ref):
    quarter = own_ref.shape[0]
    blocks = [
        own_ref[...],
        reordered(sib_ref[...], (1, 0, 3, 2)),
        reordered(far_ref[...], (2, 3, 0, 1)),
        reordered(far_sib_ref[...], (3, 2, 1, 0)),
    ]
    wide = [block.astype(jnp.float32) for block in blocks]
    total = wide[0] + wide[1] + wide[2] + wide[3]
    mean = jnp.sum(total, axis=0, keepdims=True) * (1.0 / samples)
    real = lax.broadcasted_iota(jnp.int32, wide[0].shape, 0) % PAD < rows
    squares = jnp.zeros_like(total)
    for i, block in enumerate(wide):
        centered = jnp.where(real, block - mean, 0.0).astype(jnp.bfloat16)
        c_ref[quarter * i : quarter * i + quarter, :] = centered
        centered = centered.astype(jnp.float32)
        squares += centered * centered
    sum_squares = jnp.sum(squares, axis=0, keepdims=True)
    spread_std = jnp.sqrt(sum_squares * (1.0 / (samples - 1)) + 0.0001)
    coef_var = samples / (2.0 * (samples - 1))
    hinge = jax.nn.sigmoid(10.0 * (1.0 - spread_std))
    coef_cov = 0.08 * samples / ((samples - 1) * (samples - 1))
    factor = coef_var * hinge / spread_std + coef_cov * sum_squares
    f_ref[...] = jnp.broadcast_to(factor, f_ref.shape)
    g_ref[...] = matmul(c_ref[:quarter, :], c_ref[...], 1, 1).astype(g_ref.dtype)


def total_kernel(x_ref, o_ref):
    x = x_ref[...].reshape(x_ref.shape[0] // PAD, PAD, x_ref.shape[1])
    total = jnp.sum(x.astype(jnp.float32), axis=0).astype(o_ref.dtype)
    for i in range(o_ref.shape[0] // PAD):
        o_ref[PAD * i : PAD * i + PAD, :] = total


def grad_kernel(rows, samples, m_ref, c_ref, f_ref, e_ref, p_ref, o_ref, *run_refs):
    coef_cov = 0.08 * samples / ((samples - 1) * (samples - 1))
    coupled = matmul(m_ref[...], c_ref[...], 1, 0)
    centered = c_ref[: e_ref.shape[0], :].astype(jnp.float32)
    apart = e_ref[...].astype(jnp.float32) - p_ref[...].astype(jnp.float32)
    grad = apart - f_ref[:1, :] * centered + coef_cov * coupled
    grad = grad.astype(jnp.bfloat16)
    o_ref[...] = grad
    for i, ref in enumerate(run_refs[:2]):
        ref[...] = grad[:, 128 * i : 128 * i + 128]
    packed = without_padding(grad[:, 256:], rows)
    for i, ref in enumerate(run_refs[2:]):
        ref[...] = packed[:, 128 * i : 128 * i + 128]


def hidden_kernel(g_ref, a_ref, b_ref, c_ref, d_ref, o_ref):
    w = jnp.concatenate([a_ref[...], b_ref[...], c_ref[...], d_ref[...]], axis=1)
    o_ref[...] = matmul(g_ref[...], w, 1, 1).astype(o_ref.dtype)


def weight_kernel(h0_ref, h1_ref, h2_ref, h3_ref, g0_ref, g1_ref, g2_ref, g3_ref, o_ref):
    h = jnp.concatenate([h0_ref[...], h1_ref[...], h2_ref[...], h3_ref[...]], axis=0)
    g = jnp.concatenate([g0_ref[...], g1_ref[...], g2_ref[...], g3_ref[...]], axis=0)
    o_ref[...] = matmul(h, g, 0, 0).astype(o_ref.dtype)


def copies_of(block, count):
    n = block.shape[-1]
    return pl.pallas_call(
        copies_kernel,
        out_shape=shape((count * PAD, n)),
        compiler_params=params(),
        cost_estimate=cost(0, 2 * count * PAD * n),
    )(block)


def embed(plane, weights, tile=TILE):
    rows, width = plane.shape
    units = weights[0].shape[1]
    return pl.pallas_call(
        embed_kernel,
        grid=(width // tile,),
        in_specs=[pl.BlockSpec((rows, tile), lambda k: (0, k))]
        + [pl.BlockSpec((tile, units), lambda k: (k, 0))] * 4,
        out_specs=pl.BlockSpec((rows, 4 * units), lambda k: (0, 0)),
        out_shape=shape((rows, 4 * units)),
        scratch_shapes=[pltpu.VMEM((rows, 4 * units), jnp.float32)],
        compiler_params=params(1),
        cost_estimate=cost(8 * rows * width * units, 2 * width * (rows + 4 * units)),
    )(plane, *weights)


def hidden_terms(grad, weights, tile=TILE):
    rows, units = grad.shape[0], weights[0].shape[1]
    width = weights[0].shape[0]
    return pl.pallas_call(
        hidden_kernel,
        grid=(width // tile,),
        in_specs=[pl.BlockSpec(grad.shape, lambda n: (0, 0))]
        + [pl.BlockSpec((tile, units), lambda n: (n, 0))] * 4,
        out_specs=pl.BlockSpec((rows, tile), lambda n: (0, n)),
        out_shape=shape((rows, width)),
        compiler_params=params(1),
        cost_estimate=cost(8 * rows * width * units, 2 * width * (rows + 4 * units)),
    )(grad, *weights)


def weight_terms(parts, grads, tile=TILE):
    rows, units = grads[-1].shape
    width = min(array.shape[1] for array, _ in parts)
    specs = [
        pl.BlockSpec((array.shape[0], tile), lambda n, first=first: (0, n + first))
        for array, first in parts
    ]
    return pl.pallas_call(
        weight_kernel,
        grid=(width // tile,),
        in_specs=specs + [pl.BlockSpec(g.shape, lambda n: (0, 0)) for g in grads],
        out_specs=pl.BlockSpec((tile, units), lambda n: (n, 0)),
        out_shape=shape((width, units)),
        compiler_params=params(1),
        cost_estimate=cost(8 * rows * width * units, 8 * width * rows + 2 * width * units),
    )(*[array for array, _ in parts], *grads)


def wide_sum(a, b):
    return a.astype(jnp.float32) + b.astype(jnp.float32)


def on_device(hidden, weight):
    rows = hidden.shape[1]
    width = hidden.shape[2]
    samples = rows * DP
    units = weight.shape[1]
    peers = YS * XS
    quarter = peers * PAD

    w_far = swap(weight, view=1, z=1)
    w_sib = swap(weight, c=1)
    w_far_sib = swap(w_far, c=1)
    weights = (weight, w_sib, w_far, w_far_sib)

    plane = exchange(copies_of(hidden, peers), "yx")
    plane, w_far_sib = lax.optimization_barrier((plane, w_far_sib))

    mine = embed(plane, weights)
    from_sib = swap(mine, c=1)
    from_far = swap(mine, z=1)
    from_far_sib = swap(from_far, c=1)
    partner = swap(mine, view=1)

    cuts = (0, width // 2, 3 * width // 4, width)
    late, _ = lax.optimization_barrier((plane, from_far))
    h_far = compact(late, rows, [high - low for low, high in zip(cuts, cuts[1:])])
    h_far = [swap(block, z=1) for block in h_far]
    h_sib = swap(plane, c=1)

    centered, factor, gram = pl.pallas_call(
        functools.partial(center_kernel, rows, samples),
        out_shape=(
            shape((4 * quarter, 4 * units)),
            shape((8, 4 * units), jnp.float32),
            shape((quarter, 4 * quarter)),
        ),
        compiler_params=params(),
        cost_estimate=cost(8 * 4 * quarter * quarter * units, 16 * quarter * units * 2),
    )(mine, from_sib, from_far, from_far_sib)

    gram = exchange(gram, "yx")
    gram = pl.pallas_call(
        total_kernel,
        out_shape=shape(gram.shape),
        compiler_params=params(),
        cost_estimate=cost(gram.size, 4 * gram.size),
    )(gram)
    gram, h_far[0] = lax.optimization_barrier((gram, h_far[0]))
    gram = exchange(gram, "yx")
    gram, h_far[0], h_far[1] = lax.optimization_barrier((gram, h_far[0], h_far[1]))

    grad, *runs = pl.pallas_call(
        functools.partial(grad_kernel, rows, samples),
        out_shape=(shape((quarter, 4 * units)),)
        + (shape((quarter, units)),) * 2
        + (shape((peers * rows, units)),) * 2,
        compiler_params=params(),
        cost_estimate=cost(8 * 4 * quarter * quarter * units, 16 * quarter * units * 2),
    )(gram, centered, factor, mine, partner)
    grads = (
        swap(runs[2], z=1),
        swap(runs[3], z=1, c=1),
        runs[0],
        swap(runs[1], c=1),
    )

    h_part = hidden_terms(grad, weights)
    h_part, h_far[2] = lax.optimization_barrier((h_part, h_far[2]))
    pieces = exchange(h_part, "yx").reshape(peers, PAD, width)
    grad_rows = jnp.sum(pieces.astype(jnp.float32), axis=0)[:rows]

    runs = []
    for at, far in zip(cuts, h_far):
        first = at // TILE
        total = weight_terms(
            ((far, 0), (swap(far, c=1), 0), (plane, first), (h_sib, first)), grads
        )
        runs.append(wide_sum(total, swap(total, view=1)))
    grad_weight = jnp.concatenate(runs, axis=0) / jnp.sqrt(2.0 * samples)
    return (grad_rows[None], grad_weight)


def solution(mesh):
    return jax.shard_map(
        on_device,
        mesh=mesh,
        in_specs=(P("view", "dp", None), P(None, "dp")),
        out_specs=(P("view", "dp", None), P(None, "dp")),
        check_vma=False,
    )
```

```python
import functools

import jax
import jax.numpy as jnp
from jax import lax
from jax.experimental import pallas as pl
from jax.experimental.pallas import tpu as pltpu
from jax.sharding import PartitionSpec as P

YS, ZS, XS, CS = 4, 2, 4, 2
DP = YS * ZS * XS * CS
PAD = 16
TILE = 2048
VMEM = 40 * 1024 * 1024


def place(d):
    return (d // (ZS * XS * CS), d // (XS * CS) % ZS, d // CS % XS, d % CS)


def index(y, z, x, c):
    return ((y * ZS + z) * XS + x) * CS + c


def groups(axes):
    found = {}
    for d in range(DP):
        key = tuple(p for p, name in zip(place(d), "yzxc") if name not in axes)
        found.setdefault(key, []).append(d)
    return list(found.values())


def swap(block, view=0, z=0, c=0):
    route = []
    for v in range(2):
        for d in range(DP):
            y, zd, x, cd = place(d)
            route.append((v * DP + d, (v ^ view) * DP + index(y, zd ^ z, x, cd ^ c)))
    return lax.ppermute(block, ("view", "dp"), route)


def exchange(blocks, axes):
    return lax.all_to_all(blocks, "dp", 0, 0, tiled=True, axis_index_groups=groups(axes))


def matmul(a, b, a_dim, b_dim):
    return lax.dot_general(
        a, b, (((a_dim,), (b_dim,)), ((), ())), preferred_element_type=jnp.float32
    )


def rounded(values):
    return lax.optimization_barrier(values.astype(jnp.bfloat16))


def reordered(block, order):
    return jnp.concatenate([block[:, 128 * i : 128 * i + 128] for i in order], axis=1)


def shape(dims, dtype=jnp.bfloat16):
    return jax.ShapeDtypeStruct(dims, dtype)


def params(steps=0):
    semantics = ("arbitrary",) * steps if steps else None
    return pltpu.CompilerParams(vmem_limit_bytes=VMEM, dimension_semantics=semantics)


def cost(flops, size):
    return pl.CostEstimate(flops=flops, bytes_accessed=size, transcendentals=0)


def without_padding(x, rows):
    n = x.shape[0] // PAD * rows
    out = lax.broadcasted_iota(jnp.int32, (n, x.shape[0]), 0)
    source = lax.broadcasted_iota(jnp.int32, (n, x.shape[0]), 1)
    pick = out + out // rows * (PAD - rows) == source
    return matmul(jnp.where(pick, 1.0, 0.0).astype(x.dtype), x, 1, 0).astype(x.dtype)


def compact_kernel(rows, x_ref, *o_refs):
    at = 0
    for ref in o_refs:
        n = ref.shape[1]
        ref[...] = without_padding(x_ref[:, at : at + n], rows)
        at += n


def compact(block, rows, widths):
    n = block.shape[0] // PAD * rows
    return pl.pallas_call(
        functools.partial(compact_kernel, rows),
        out_shape=tuple(shape((n, width)) for width in widths),
        compiler_params=params(),
        cost_estimate=cost(2 * n * block.size, 4 * block.size),
    )(block)


def copies_kernel(x_ref, o_ref):
    x = x_ref[0]
    zeros = jnp.zeros((PAD - x.shape[0], x.shape[1]), x.dtype)
    x = jnp.concatenate([x, zeros], axis=0)
    for i in range(o_ref.shape[0] // PAD):
        o_ref[PAD * i : PAD * i + PAD, :] = x


def embed_kernel(h_ref, a_ref, b_ref, c_ref, d_ref, o_ref, acc_ref):
    step = pl.program_id(0)

    @pl.when(step == 0)
    def _():
        acc_ref[...] = jnp.zeros_like(acc_ref)

    w = jnp.concatenate([a_ref[...], b_ref[...], c_ref[...], d_ref[...]], axis=1)
    acc_ref[...] += matmul(h_ref[...], w, 1, 0)

    @pl.when(step == pl.num_programs(0) - 1)
    def _():
        o_ref[...] = acc_ref[...].astype(o_ref.dtype)


def center_kernel(rows, samples, own_ref, sib_ref, far_ref, far_sib_ref, c_ref, f_ref, g_ref):
    quarter = own_ref.shape[0]
    blocks = [
        own_ref[...],
        reordered(sib_ref[...], (1, 0, 3, 2)),
        reordered(far_ref[...], (2, 3, 0, 1)),
        reordered(far_sib_ref[...], (3, 2, 1, 0)),
    ]
    wide = [block.astype(jnp.float32) for block in blocks]
    total = wide[0] + wide[1] + wide[2] + wide[3]
    mean = jnp.sum(total, axis=0, keepdims=True) * (1.0 / samples)
    real = lax.broadcasted_iota(jnp.int32, wide[0].shape, 0) % PAD < rows
    squares = jnp.zeros_like(total)
    for i, block in enumerate(wide):
        centered = jnp.where(real, block - mean, 0.0).astype(jnp.bfloat16)
        c_ref[quarter * i : quarter * i + quarter, :] = centered
        centered = centered.astype(jnp.float32)
        squares += centered * centered
    sum_squares = jnp.sum(squares, axis=0, keepdims=True)
    spread_std = jnp.sqrt(sum_squares * (1.0 / (samples - 1)) + 0.0001)
    coef_var = samples / (2.0 * (samples - 1))
    hinge = jax.nn.sigmoid(10.0 * (1.0 - spread_std))
    coef_cov = 0.08 * samples / ((samples - 1) * (samples - 1))
    factor = coef_var * hinge / spread_std + coef_cov * sum_squares
    f_ref[...] = jnp.broadcast_to(factor, f_ref.shape)
    g_ref[...] = matmul(c_ref[:quarter, :], c_ref[...], 1, 1).astype(g_ref.dtype)


def total_kernel(x_ref, o_ref):
    x = x_ref[...].reshape(x_ref.shape[0] // PAD, PAD, x_ref.shape[1])
    total = jnp.sum(x.astype(jnp.float32), axis=0).astype(o_ref.dtype)
    for i in range(o_ref.shape[0] // PAD):
        o_ref[PAD * i : PAD * i + PAD, :] = total


def grad_kernel(rows, samples, m_ref, c_ref, f_ref, e_ref, p_ref, o_ref, *run_refs):
    coef_cov = 0.08 * samples / ((samples - 1) * (samples - 1))
    coupled = matmul(m_ref[...], c_ref[...], 1, 0)
    centered = c_ref[: e_ref.shape[0], :].astype(jnp.float32)
    apart = e_ref[...].astype(jnp.float32) - p_ref[...].astype(jnp.float32)
    grad = apart - f_ref[:1, :] * centered + coef_cov * coupled
    grad = grad.astype(jnp.bfloat16)
    o_ref[...] = grad
    own_ref, far_ref = run_refs
    n = own_ref.shape[1]
    own_ref[...] = grad[:, :n]
    far_ref[...] = without_padding(grad[:, n:], rows)


def hidden_kernel(g_ref, a_ref, b_ref, c_ref, d_ref, o_ref):
    w = jnp.concatenate([a_ref[...], b_ref[...], c_ref[...], d_ref[...]], axis=1)
    o_ref[...] = matmul(g_ref[...], w, 1, 1).astype(o_ref.dtype)


def weight_kernel(low, n_far, *refs):
    fars, (own_ref, gf_ref, go_ref, mine_ref, sib_ref) = refs[:n_far], refs[n_far:]
    n = mine_ref.shape[0]
    far = jnp.concatenate([ref[...] for ref in fars], axis=1)
    h = jnp.concatenate([own_ref[:, low : low + n], far], axis=0)
    g = jnp.concatenate([go_ref[...], gf_ref[...]], axis=0)
    out = matmul(h, g, 0, 0)
    units = mine_ref.shape[1]
    mine_ref[...] = out[:, :units]
    sib_ref[...] = out[:, units:].astype(sib_ref.dtype)


def copies_of(block, count):
    n = block.shape[-1]
    return pl.pallas_call(
        copies_kernel,
        out_shape=shape((count * PAD, n)),
        compiler_params=params(),
        cost_estimate=cost(0, 2 * count * PAD * n),
    )(block)


def embed(plane, weights, tile=TILE):
    rows, width = plane.shape
    units = weights[0].shape[1]
    return pl.pallas_call(
        embed_kernel,
        grid=(width // tile,),
        in_specs=[pl.BlockSpec((rows, tile), lambda k: (0, k))]
        + [pl.BlockSpec((tile, units), lambda k: (k, 0))] * 4,
        out_specs=pl.BlockSpec((rows, 4 * units), lambda k: (0, 0)),
        out_shape=shape((rows, 4 * units)),
        scratch_shapes=[pltpu.VMEM((rows, 4 * units), jnp.float32)],
        compiler_params=params(1),
        cost_estimate=cost(8 * rows * width * units, 2 * width * (rows + 4 * units)),
    )(plane, *weights)


def hidden_terms(grad, weights, tile=TILE):
    rows, units = grad.shape[0], weights[0].shape[1]
    width = weights[0].shape[0]
    return pl.pallas_call(
        hidden_kernel,
        grid=(width // tile,),
        in_specs=[pl.BlockSpec(grad.shape, lambda n: (0, 0))]
        + [pl.BlockSpec((tile, units), lambda n: (n, 0))] * 4,
        out_specs=pl.BlockSpec((rows, tile), lambda n: (0, n)),
        out_shape=shape((rows, width)),
        compiler_params=params(1),
        cost_estimate=cost(8 * rows * width * units, 2 * width * (rows + 4 * units)),
    )(grad, *weights)


def weight_terms(plane, low, fars, g_far, g_own):
    rows = plane.shape[0]
    width = sum(far.shape[1] for far in fars)
    units = g_own.shape[1] // 2
    return pl.pallas_call(
        functools.partial(weight_kernel, low, len(fars)),
        out_shape=(shape((width, units), jnp.float32), shape((width, units))),
        compiler_params=params(),
        cost_estimate=cost(8 * rows * width * units, 4 * width * (rows + 2 * units)),
    )(*fars, plane, g_far, g_own)


def wide_sum(a, b):
    return a.astype(jnp.float32) + b.astype(jnp.float32)


def on_device(hidden, weight):
    rows = hidden.shape[1]
    width = hidden.shape[2]
    samples = rows * DP
    units = weight.shape[1]
    peers = YS * XS
    quarter = peers * PAD

    w_far = swap(weight, view=1, z=1)
    w_sib = swap(weight, c=1)
    w_far_sib = swap(w_far, c=1)
    weights = (weight, w_sib, w_far, w_far_sib)

    plane = exchange(copies_of(hidden, peers), "yx")
    plane, w_far_sib = lax.optimization_barrier((plane, w_far_sib))

    mine = embed(plane, weights)
    from_sib = swap(mine, c=1)
    from_far = swap(mine, z=1)
    from_far_sib = swap(from_far, c=1)
    partner = swap(mine, view=1)

    cuts = (0, width // 2, 7 * width // 8, width)
    late, _ = lax.optimization_barrier((plane, from_far))
    h_far = compact(late, rows, [high - low for low, high in zip(cuts, cuts[1:])])
    h_far = [swap(block, z=1) for block in h_far]

    centered, factor, gram = pl.pallas_call(
        functools.partial(center_kernel, rows, samples),
        out_shape=(
            shape((4 * quarter, 4 * units)),
            shape((8, 4 * units), jnp.float32),
            shape((quarter, 4 * quarter)),
        ),
        compiler_params=params(),
        cost_estimate=cost(8 * 4 * quarter * quarter * units, 16 * quarter * units * 2),
    )(mine, from_sib, from_far, from_far_sib)

    gram = exchange(gram, "yx")
    gram, partner = lax.optimization_barrier((gram, partner))
    gram = pl.pallas_call(
        total_kernel,
        out_shape=shape(gram.shape),
        compiler_params=params(),
        cost_estimate=cost(gram.size, 4 * gram.size),
    )(gram)
    gram, h_far[0] = lax.optimization_barrier((gram, h_far[0]))
    gram = exchange(gram, "yx")
    gram, h_far[0], h_far[1] = lax.optimization_barrier((gram, h_far[0], h_far[1]))

    grad, g_own, g_far = pl.pallas_call(
        functools.partial(grad_kernel, rows, samples),
        out_shape=(shape((quarter, 4 * units)),)
        + (shape((quarter, 2 * units)), shape((peers * rows, 2 * units))),
        compiler_params=params(),
        cost_estimate=cost(8 * 4 * quarter * quarter * units, 16 * quarter * units * 2),
    )(gram, centered, factor, mine, partner)
    g_far = swap(g_far, z=1)

    h_part = hidden_terms(grad, weights)
    h_part, h_far[2] = lax.optimization_barrier((h_part, h_far[2]))
    pieces = exchange(h_part, "yx").reshape(peers, PAD, width)
    grad_rows = jnp.sum(pieces.astype(jnp.float32), axis=0)[:rows]

    runs = []
    for low, fars in ((0, h_far[:1]), (cuts[1], h_far[1:])):
        mine, theirs = weight_terms(plane, low, fars, g_far, g_own)
        total = rounded(mine + swap(theirs, c=1).astype(jnp.float32))
        runs.append(wide_sum(total, swap(total, view=1)))
    grad_weight = jnp.concatenate(runs, axis=0) / jnp.sqrt(2.0 * samples)
    return (grad_rows[None], grad_weight)


def solution(mesh):
    return jax.shard_map(
        on_device,
        mesh=mesh,
        in_specs=(P("view", "dp", None), P(None, "dp")),
        out_specs=(P("view", "dp", None), P(None, "dp")),
        check_vma=False,
    )
```

```python
import functools

import jax
import jax.numpy as jnp
from jax import lax
from jax.experimental import pallas as pl
from jax.experimental.pallas import tpu as pltpu
from jax.sharding import PartitionSpec as P

YS, ZS, XS, CS = 4, 2, 4, 2
DP = YS * ZS * XS * CS
PAD = 16
TILE = 2048
VMEM = 24 * 1024 * 1024


def place(d):
    return (d // (ZS * XS * CS), d // (XS * CS) % ZS, d // CS % XS, d % CS)


def index(y, z, x, c):
    return ((y * ZS + z) * XS + x) * CS + c


def groups(axes):
    found = {}
    for d in range(DP):
        key = tuple(p for p, name in zip(place(d), "yzxc") if name not in axes)
        found.setdefault(key, []).append(d)
    return list(found.values())


def swap(block, view=0, z=0, c=0):
    route = []
    for v in range(2):
        for d in range(DP):
            y, zd, x, cd = place(d)
            route.append((v * DP + d, (v ^ view) * DP + index(y, zd ^ z, x, cd ^ c)))
    return lax.ppermute(block, ("view", "dp"), route)


def exchange(blocks, axes):
    return lax.all_to_all(blocks, "dp", 0, 0, tiled=True, axis_index_groups=groups(axes))


def matmul(a, b, a_dim, b_dim):
    return lax.dot_general(
        a, b, (((a_dim,), (b_dim,)), ((), ())), preferred_element_type=jnp.float32
    )


def rounded(values):
    return lax.optimization_barrier(values.astype(jnp.bfloat16))


def reordered(block, order):
    return jnp.concatenate([block[:, 128 * i : 128 * i + 128] for i in order], axis=1)


def shape(dims, dtype=jnp.bfloat16):
    return jax.ShapeDtypeStruct(dims, dtype)


def params(steps=0):
    semantics = ("arbitrary",) * steps if steps else None
    return pltpu.CompilerParams(vmem_limit_bytes=VMEM, dimension_semantics=semantics)


def cost(flops, size):
    return pl.CostEstimate(flops=flops // 1000, bytes_accessed=size // 1000, transcendentals=0)


def without_padding(x, rows):
    n = x.shape[0] // PAD * rows
    out = lax.broadcasted_iota(jnp.int32, (n, x.shape[0]), 0)
    source = lax.broadcasted_iota(jnp.int32, (n, x.shape[0]), 1)
    pick = out + out // rows * (PAD - rows) == source
    return matmul(jnp.where(pick, 1.0, 0.0).astype(x.dtype), x, 1, 0).astype(x.dtype)


def compact_kernel(rows, x_ref, *o_refs):
    at = x_ref.shape[1] - sum(ref.shape[1] for ref in o_refs)
    for ref in o_refs:
        n = ref.shape[1]
        ref[...] = without_padding(x_ref[:, at : at + n], rows)
        at += n


def compact(block, rows, widths):
    n = block.shape[0] // PAD * rows
    return pl.pallas_call(
        functools.partial(compact_kernel, rows),
        out_shape=tuple(shape((n, width)) for width in widths),
        compiler_params=params(),
        cost_estimate=cost(2 * n * block.shape[0] * sum(widths), 4 * block.size),
    )(block)


def pad_rows(blocks):
    zeros = jnp.zeros((PAD - blocks[0].shape[0], blocks[0].shape[1]), blocks[0].dtype)
    return jnp.concatenate([part for block in blocks for part in (block, zeros)], axis=0)


def settle_kernel(rows, at_ref, *refs):
    blocks, (o_ref, all_ref) = refs[:YS], refs[YS:]
    for i, ref in enumerate(blocks):
        y = lax.rem(at_ref[0] + (YS - i), YS)
        for j in range(XS):
            x = lax.rem(at_ref[1] + (XS - j), XS)
            home = pl.multiple_of((y * XS + x) * PAD, PAD)
            all_ref[pl.ds(home, PAD), :] = ref[PAD * j : PAD * j + PAD, :]
    o_ref[...] = without_padding(all_ref[...], rows)


def settle(at, blocks, rows):
    n, width = YS * XS * PAD, blocks[0].shape[1]
    return pl.pallas_call(
        functools.partial(settle_kernel, rows),
        in_specs=[pl.BlockSpec(memory_space=pltpu.SMEM)]
        + [pl.BlockSpec(memory_space=pltpu.VMEM)] * YS,
        out_shape=shape((YS * XS * rows, width)),
        scratch_shapes=[pltpu.VMEM((n, width), jnp.bfloat16)],
        compiler_params=params(),
        cost_estimate=cost(2 * n * n * width, 4 * n * width),
    )(at, *blocks)


def copies_kernel(x_ref, o_ref):
    x = x_ref[0]
    zeros = jnp.zeros((PAD - x.shape[0], x.shape[1]), x.dtype)
    x = jnp.concatenate([x, zeros], axis=0)
    for i in range(o_ref.shape[0] // PAD):
        o_ref[PAD * i : PAD * i + PAD, :] = x


def embed_kernel(h_ref, a_ref, b_ref, c_ref, d_ref, o_ref, acc_ref):
    step = pl.program_id(0)

    @pl.when(step == 0)
    def _():
        acc_ref[...] = jnp.zeros_like(acc_ref)

    w = jnp.concatenate([a_ref[...], b_ref[...], c_ref[...], d_ref[...]], axis=1)
    acc_ref[...] += matmul(h_ref[...], w, 1, 0)

    @pl.when(step == pl.num_programs(0) - 1)
    def _():
        o_ref[...] = acc_ref[...].astype(o_ref.dtype)


def center_kernel(rows, samples, own_ref, sib_ref, far_ref, far_sib_ref, c_ref, f_ref, g_ref):
    quarter = own_ref.shape[0]
    blocks = [
        own_ref[...],
        reordered(sib_ref[...], (1, 0, 3, 2)),
        reordered(far_ref[...], (2, 3, 0, 1)),
        reordered(far_sib_ref[...], (3, 2, 1, 0)),
    ]
    wide = [block.astype(jnp.float32) for block in blocks]
    total = wide[0] + wide[1] + wide[2] + wide[3]
    mean = jnp.sum(total, axis=0, keepdims=True) * (1.0 / samples)
    real = lax.broadcasted_iota(jnp.int32, wide[0].shape, 0) % PAD < rows
    squares = jnp.zeros_like(total)
    for i, block in enumerate(wide):
        centered = jnp.where(real, block - mean, 0.0).astype(jnp.bfloat16)
        c_ref[quarter * i : quarter * i + quarter, :] = centered
        centered = centered.astype(jnp.float32)
        squares += centered * centered
    sum_squares = jnp.sum(squares, axis=0, keepdims=True)
    spread_std = jnp.sqrt(sum_squares * (1.0 / (samples - 1)) + 0.0001)
    coef_var = samples / (2.0 * (samples - 1))
    hinge = jax.nn.sigmoid(10.0 * (1.0 - spread_std))
    coef_cov = 0.08 * samples / ((samples - 1) * (samples - 1))
    factor = coef_var * hinge / spread_std + coef_cov * sum_squares
    f_ref[...] = jnp.broadcast_to(factor, f_ref.shape)
    g_ref[...] = matmul(c_ref[:quarter, :], c_ref[...], 1, 1).astype(g_ref.dtype)


def total_kernel(x_ref, o_ref):
    x = x_ref[...].reshape(x_ref.shape[0] // PAD, PAD, x_ref.shape[1])
    total = jnp.sum(x.astype(jnp.float32), axis=0).astype(o_ref.dtype)
    for i in range(o_ref.shape[0] // PAD):
        o_ref[PAD * i : PAD * i + PAD, :] = total


def grad_kernel(rows, samples, m_ref, c_ref, f_ref, e_ref, p_ref, o_ref, *run_refs):
    coef_cov = 0.08 * samples / ((samples - 1) * (samples - 1))
    coupled = matmul(m_ref[...], c_ref[...], 1, 0)
    centered = c_ref[: e_ref.shape[0], :].astype(jnp.float32)
    apart = e_ref[...].astype(jnp.float32) - p_ref[...].astype(jnp.float32)
    grad = apart - f_ref[:1, :] * centered + coef_cov * coupled
    grad = grad.astype(jnp.bfloat16)
    o_ref[...] = grad
    packed = without_padding(grad[:, 256:], rows)
    for i, ref in enumerate(run_refs[:2]):
        ref[...] = grad[:, 128 * i : 128 * i + 128]
    for i, ref in enumerate(run_refs[2:]):
        ref[...] = packed[:, 128 * i : 128 * i + 128]


def hidden_kernel(g_ref, a_ref, b_ref, c_ref, d_ref, o_ref):
    w = jnp.concatenate([a_ref[...], b_ref[...], c_ref[...], d_ref[...]], axis=1)
    o_ref[...] = matmul(g_ref[...], w, 1, 1).astype(o_ref.dtype)


def weight_kernel(low, n_far, *refs):
    fars, sibs, (own_ref, sib_ref), gs, (o_ref,) = (
        refs[:n_far],
        refs[n_far : 2 * n_far],
        refs[2 * n_far : 2 * n_far + 2],
        refs[2 * n_far + 2 : -1],
        refs[-1:],
    )
    n = o_ref.shape[0]
    h = jnp.concatenate(
        [
            own_ref[:, low : low + n],
            sib_ref[:, low : low + n],
            jnp.concatenate([ref[...] for ref in fars], axis=1),
            jnp.concatenate([ref[...] for ref in sibs], axis=1),
        ],
        axis=0,
    )
    g = jnp.concatenate([ref[...] for ref in gs], axis=0)
    o_ref[...] = matmul(h, g, 0, 0).astype(o_ref.dtype)


def copies_of(block, count):
    n = block.shape[-1]
    return pl.pallas_call(
        copies_kernel,
        out_shape=shape((count * PAD, n)),
        compiler_params=params(),
        cost_estimate=cost(0, 2 * count * PAD * n),
    )(block)


def embed(plane, weights, tile=TILE):
    rows, width = plane.shape
    units = weights[0].shape[1]
    return pl.pallas_call(
        embed_kernel,
        grid=(width // tile,),
        in_specs=[pl.BlockSpec((rows, tile), lambda k: (0, k))]
        + [pl.BlockSpec((tile, units), lambda k: (k, 0))] * 4,
        out_specs=pl.BlockSpec((rows, 4 * units), lambda k: (0, 0)),
        out_shape=shape((rows, 4 * units)),
        scratch_shapes=[pltpu.VMEM((rows, 4 * units), jnp.float32)],
        compiler_params=params(1),
        cost_estimate=cost(8 * rows * width * units, 2 * width * (rows + 4 * units)),
    )(plane, *weights)


def hidden_terms(grad, weights, tile=TILE):
    rows, units = grad.shape[0], weights[0].shape[1]
    width = weights[0].shape[0]
    return pl.pallas_call(
        hidden_kernel,
        grid=(width // tile,),
        in_specs=[pl.BlockSpec(grad.shape, lambda n: (0, 0))]
        + [pl.BlockSpec((tile, units), lambda n: (n, 0))] * 4,
        out_specs=pl.BlockSpec((rows, tile), lambda n: (0, n)),
        out_shape=shape((rows, width)),
        compiler_params=params(1),
        cost_estimate=cost(8 * rows * width * units, 2 * width * (rows + 4 * units)),
    )(grad, *weights)


def weight_terms(low, fars, sibs, plane, h_sib, grads):
    width = sum(far.shape[1] for far in fars)
    units = grads[0].shape[1]
    rows = 4 * plane.shape[0]
    return pl.pallas_call(
        functools.partial(weight_kernel, low, len(fars)),
        out_shape=shape((width, units)),
        compiler_params=params(),
        cost_estimate=cost(2 * rows * width * units, 2 * width * (rows + units)),
    )(*fars, *sibs, plane, h_sib, *grads)


def wide_sum(a, b):
    return a.astype(jnp.float32) + b.astype(jnp.float32)


def shift(block, y=0, x=0):
    route = []
    for d in range(DP):
        yd, z, xd, c = place(d)
        route.append((d, index((yd + y) % YS, z, (xd + x) % XS, c)))
    return lax.ppermute(block, "dp", route)


def on_device(hidden, weight):
    rows = hidden.shape[1]
    width = hidden.shape[2]
    samples = rows * DP
    units = weight.shape[1]
    peers = YS * XS
    quarter = peers * PAD

    w_far = swap(weight, view=1, z=1)
    w_sib = swap(weight, c=1)
    w_far_sib = swap(w_far, c=1)
    weights = (weight, w_sib, w_far, w_far_sib)

    d = lax.axis_index("dp")
    at = jnp.stack([d // (ZS * XS * CS), d // CS % XS]).astype(jnp.int32)
    far = swap(hidden[0, :, : width // 2], z=1)
    far = pad_rows([far] + [shift(far, x=k) for k in (1, 2, 3)])

    plane = exchange(copies_of(hidden, peers), "yx")
    plane, w_far_sib, far = lax.optimization_barrier((plane, w_far_sib, far))

    mine = embed(plane, weights)
    from_sib = swap(mine, c=1)
    from_far = swap(mine, z=1)
    from_far_sib = swap(from_far, c=1)
    partner = swap(mine, view=1)

    far, _ = lax.optimization_barrier((far, mine))
    far = [far] + [shift(far, y=k) for k in (1, 2, 3)]
    h_right = compact(plane, rows, (width // 4, width // 4))
    *h_right, from_far_sib, _, _ = lax.optimization_barrier(
        (*h_right, from_far_sib, from_far, from_sib)
    )
    h_right = [swap(block, z=1) for block in h_right]

    centered, factor, gram = pl.pallas_call(
        functools.partial(center_kernel, rows, samples),
        out_shape=(
            shape((4 * quarter, 4 * units)),
            shape((8, 4 * units), jnp.float32),
            shape((quarter, 4 * quarter)),
        ),
        compiler_params=params(),
        cost_estimate=cost(8 * 4 * quarter * quarter * units, 16 * quarter * units * 2),
    )(mine, from_sib, from_far, from_far_sib)

    gram, *far = lax.optimization_barrier((gram, *far))
    gram = exchange(gram, "yx")
    h_left = settle(at, far, rows)
    gram, partner, plane_late, h_left, h_right[0] = lax.optimization_barrier(
        (gram, partner, plane, h_left, h_right[0])
    )
    h_left_sib = [swap(h_left, c=1)]
    h_sib = swap(plane_late, c=1)
    gram = pl.pallas_call(
        total_kernel,
        out_shape=shape(gram.shape),
        compiler_params=params(),
        cost_estimate=cost(gram.size, 4 * gram.size),
    )(gram)
    gram = exchange(gram, "yx")
    gram, *h_right, h_left_sib[0], h_sib = lax.optimization_barrier(
        (gram, *h_right, h_left_sib[0], h_sib)
    )
    h_right_sib = [swap(block, c=1) for block in h_right]

    grad, *runs = pl.pallas_call(
        functools.partial(grad_kernel, rows, samples),
        out_shape=(shape((quarter, 4 * units)),)
        + (shape((quarter, units)),) * 2
        + (shape((peers * rows, units)),) * 2,
        compiler_params=params(),
        cost_estimate=cost(8 * 4 * quarter * quarter * units, 16 * quarter * units * 2),
    )(gram, centered, factor, mine, partner)
    grads = (runs[0], swap(runs[1], c=1), swap(runs[2], z=1), swap(runs[3], z=1, c=1))

    h_part = hidden_terms(grad, weights)
    h_part, *grads = lax.optimization_barrier((h_part, *grads))
    pieces = exchange(h_part, "yx").reshape(peers, PAD, width)
    grad_rows = jnp.sum(pieces.astype(jnp.float32), axis=0)[:rows]

    runs = []
    for low, fars, sibs in ((0, [h_left], h_left_sib), (width // 2, h_right, h_right_sib)):
        total = weight_terms(low, fars, sibs, plane, h_sib, grads)
        runs.append(wide_sum(total, swap(total, view=1)))
    grad_weight = jnp.concatenate(runs, axis=0) / jnp.sqrt(2.0 * samples)
    return (grad_rows[None], grad_weight)


def solution(mesh):
    return jax.shard_map(
        on_device,
        mesh=mesh,
        in_specs=(P("view", "dp", None), P(None, "dp")),
        out_specs=(P("view", "dp", None), P(None, "dp")),
        check_vma=False,
    )
```

```python
import functools

import jax
import jax.numpy as jnp
from jax import lax
from jax.experimental import pallas as pl
from jax.experimental.pallas import tpu as pltpu
from jax.sharding import PartitionSpec as P

YS, ZS, XS, CS = 4, 2, 4, 2
DP = YS * ZS * XS * CS
PAD = 16
TILE = 1024
VMEM = 24 * 1024 * 1024


def place(d):
    return (d // (ZS * XS * CS), d // (XS * CS) % ZS, d // CS % XS, d % CS)


def index(y, z, x, c):
    return ((y * ZS + z) * XS + x) * CS + c


def groups(axes):
    found = {}
    for d in range(DP):
        key = tuple(p for p, name in zip(place(d), "yzxc") if name not in axes)
        found.setdefault(key, []).append(d)
    return list(found.values())


def swap(block, view=0, z=0, c=0):
    route = []
    for v in range(2):
        for d in range(DP):
            y, zd, x, cd = place(d)
            route.append((v * DP + d, (v ^ view) * DP + index(y, zd ^ z, x, cd ^ c)))
    return lax.ppermute(block, ("view", "dp"), route)


def exchange(blocks, axes):
    return lax.all_to_all(blocks, "dp", 0, 0, tiled=True, axis_index_groups=groups(axes))


def matmul(a, b, a_dim, b_dim):
    return lax.dot_general(
        a, b, (((a_dim,), (b_dim,)), ((), ())), preferred_element_type=jnp.float32
    )


def rounded(values):
    return lax.optimization_barrier(values.astype(jnp.bfloat16))


def reordered(block, order):
    return jnp.concatenate([block[:, 128 * i : 128 * i + 128] for i in order], axis=1)


def shape(dims, dtype=jnp.bfloat16):
    return jax.ShapeDtypeStruct(dims, dtype)


def params(steps):
    return pltpu.CompilerParams(
        vmem_limit_bytes=VMEM, dimension_semantics=("arbitrary",) * steps
    )


def cost(flops, size):
    return pl.CostEstimate(flops=flops, bytes_accessed=size, transcendentals=0)


def without_padding(x, rows):
    n = x.shape[0] // PAD * rows
    out = lax.broadcasted_iota(jnp.int32, (n, x.shape[0]), 0)
    source = lax.broadcasted_iota(jnp.int32, (n, x.shape[0]), 1)
    pick = out + out // rows * (PAD - rows) == source
    return matmul(jnp.where(pick, 1.0, 0.0).astype(x.dtype), x, 1, 0).astype(x.dtype)


def whole(*dims):
    return pl.BlockSpec(dims, lambda *_: (0,) * len(dims))


def columns(array_or_shape):
    peers, _, rows, tile = array_or_shape.shape
    return pl.BlockSpec((peers, 1, rows, tile), lambda k: (0, k, 0, 0))


def joined(ref):
    return ref[...].reshape(ref.shape[0] * ref.shape[2], ref.shape[3])


def compact_kernel(rows, x_ref, left_ref, right_ref):
    k = pl.program_id(0)
    packed = without_padding(joined(x_ref), rows)

    @pl.when(k < pl.num_programs(0) // 2)
    def _():
        left_ref[...] = packed

    @pl.when(k >= pl.num_programs(0) // 2)
    def _():
        right_ref[...] = packed


def compact(plane, rows):
    peers, blocks, _, tile = plane.shape
    half = blocks // 2
    out = shape((peers * rows, half * tile))
    return pl.pallas_call(
        functools.partial(compact_kernel, rows),
        grid=(blocks,),
        in_specs=[columns(plane)],
        out_specs=(
            pl.BlockSpec((peers * rows, tile), lambda k: (0, jnp.minimum(k, half - 1))),
            pl.BlockSpec((peers * rows, tile), lambda k: (0, jnp.maximum(k, half) - half)),
        ),
        out_shape=(out, out),
        compiler_params=params(1),
        cost_estimate=cost(4 * plane.size, 4 * plane.size),
    )(plane)


def copies_kernel(x_ref, o_ref):
    x = x_ref[0]
    zeros = jnp.zeros((PAD - x.shape[0], x.shape[1]), x.dtype)
    x = jnp.concatenate([x, zeros], axis=0)
    for k in range(o_ref.shape[1]):
        block = x[:, TILE * k : TILE * k + TILE]
        for i in range(o_ref.shape[0]):
            o_ref[i, k] = block


def embed_kernel(h_ref, a_ref, b_ref, c_ref, d_ref, o_ref, acc_ref):
    step = pl.program_id(0)

    @pl.when(step == 0)
    def _():
        acc_ref[...] = jnp.zeros_like(acc_ref)

    w = jnp.concatenate([a_ref[...], b_ref[...], c_ref[...], d_ref[...]], axis=1)
    acc_ref[...] += matmul(joined(h_ref), w, 1, 0)

    @pl.when(step == pl.num_programs(0) - 1)
    def _():
        o_ref[...] = acc_ref[...].astype(o_ref.dtype)


def center_kernel(rows, samples, own_ref, sib_ref, far_ref, far_sib_ref, c_ref, f_ref, g_ref):
    quarter = own_ref.shape[0]
    blocks = [
        own_ref[...],
        reordered(sib_ref[...], (1, 0, 3, 2)),
        reordered(far_ref[...], (2, 3, 0, 1)),
        reordered(far_sib_ref[...], (3, 2, 1, 0)),
    ]
    wide = [block.astype(jnp.float32) for block in blocks]
    total = wide[0] + wide[1] + wide[2] + wide[3]
    mean = jnp.sum(total, axis=0, keepdims=True) * (1.0 / samples)
    real = lax.broadcasted_iota(jnp.int32, wide[0].shape, 0) % PAD < rows
    squares = jnp.zeros_like(total)
    for i, block in enumerate(wide):
        centered = jnp.where(real, block - mean, 0.0).astype(jnp.bfloat16)
        c_ref[quarter * i : quarter * i + quarter, :] = centered
        centered = centered.astype(jnp.float32)
        squares += centered * centered
    sum_squares = jnp.sum(squares, axis=0, keepdims=True)
    spread_std = jnp.sqrt(sum_squares * (1.0 / (samples - 1)) + 0.0001)
    coef_var = samples / (2.0 * (samples - 1))
    hinge = jax.nn.sigmoid(10.0 * (1.0 - spread_std))
    coef_cov = 0.08 * samples / ((samples - 1) * (samples - 1))
    factor = coef_var * hinge / spread_std + coef_cov * sum_squares
    f_ref[...] = jnp.broadcast_to(factor, f_ref.shape)
    g_ref[...] = matmul(c_ref[:quarter, :], c_ref[...], 1, 1).astype(g_ref.dtype)


def total_kernel(x_ref, o_ref):
    x = x_ref[...].reshape(x_ref.shape[0] // PAD, PAD, x_ref.shape[1])
    total = jnp.sum(x.astype(jnp.float32), axis=0).astype(o_ref.dtype)
    for i in range(o_ref.shape[0] // PAD):
        o_ref[PAD * i : PAD * i + PAD, :] = total


def grad_kernel(rows, samples, m_ref, c_ref, f_ref, e_ref, p_ref, o_ref, *run_refs):
    coef_cov = 0.08 * samples / ((samples - 1) * (samples - 1))
    coupled = matmul(m_ref[...], c_ref[...], 1, 0)
    centered = c_ref[: e_ref.shape[0], :].astype(jnp.float32)
    apart = e_ref[...].astype(jnp.float32) - p_ref[...].astype(jnp.float32)
    grad = apart - f_ref[:1, :] * centered + coef_cov * coupled
    grad = grad.astype(jnp.bfloat16)
    o_ref[...] = grad
    own_ref, far_ref = run_refs
    n = own_ref.shape[1]
    own_ref[...] = grad[:, :n]
    far_ref[...] = without_padding(grad[:, n:], rows)


def hidden_kernel(g_ref, a_ref, b_ref, c_ref, d_ref, o_ref):
    w = jnp.concatenate([a_ref[...], b_ref[...], c_ref[...], d_ref[...]], axis=1)
    o_ref[...] = matmul(g_ref[...], w, 1, 1).astype(o_ref.dtype).reshape(o_ref.shape)


def weight_kernel(own_ref, far_ref, go_ref, gf_ref, mine_ref, sib_ref):
    h = jnp.concatenate([joined(own_ref), far_ref[...]], axis=0)
    g = jnp.concatenate([go_ref[...], gf_ref[...]], axis=0)
    out = matmul(h, g, 0, 0)
    units = mine_ref.shape[1]
    mine_ref[...] = out[:, :units]
    sib_ref[...] = out[:, units:].astype(sib_ref.dtype)


def rows_kernel(x_ref, o_ref):
    total = jnp.sum(x_ref[:, 0].astype(jnp.float32), axis=0)
    o_ref[0] = total[: o_ref.shape[1]]


def copies_of(block, count):
    out = shape((count, block.shape[2] // TILE, PAD, TILE))
    return pl.pallas_call(
        copies_kernel,
        grid=(1,),
        in_specs=[whole(*block.shape)],
        out_specs=whole(*out.shape),
        out_shape=out,
        compiler_params=params(1),
        cost_estimate=cost(0, 2 * count * block.size),
    )(block)


def embed(plane, weights):
    width, units = weights[0].shape
    rows = plane.size // width
    return pl.pallas_call(
        embed_kernel,
        grid=(width // TILE,),
        in_specs=[columns(plane)] + [pl.BlockSpec((TILE, units), lambda k: (k, 0))] * 4,
        out_specs=whole(rows, 4 * units),
        out_shape=shape((rows, 4 * units)),
        scratch_shapes=[pltpu.VMEM((rows, 4 * units), jnp.float32)],
        compiler_params=params(1),
        cost_estimate=cost(8 * rows * width * units, 2 * width * (rows + 4 * units)),
    )(plane, *weights)


def hidden_terms(grad, weights):
    rows = grad.shape[0]
    width, units = weights[0].shape
    out = shape((rows // PAD, width // TILE, PAD, TILE))
    return pl.pallas_call(
        hidden_kernel,
        grid=(width // TILE,),
        in_specs=[whole(*grad.shape)] + [pl.BlockSpec((TILE, units), lambda k: (k, 0))] * 4,
        out_specs=columns(out),
        out_shape=out,
        compiler_params=params(1),
        cost_estimate=cost(8 * rows * width * units, 2 * width * (rows + 4 * units)),
    )(grad, *weights)


def hidden_rows(pieces, rows):
    peers, blocks, _, tile = pieces.shape
    return pl.pallas_call(
        rows_kernel,
        grid=(blocks,),
        in_specs=[columns(pieces)],
        out_specs=pl.BlockSpec((1, rows, tile), lambda k: (0, 0, k)),
        out_shape=shape((1, rows, blocks * tile), jnp.float32),
        compiler_params=params(1),
        cost_estimate=cost(pieces.size, 3 * pieces.size),
    )(pieces)


def weight_terms(plane, first, far, g_own, g_far):
    peers, _, rows, tile = plane.shape
    width = far.shape[1]
    units = g_own.shape[1] // 2
    return pl.pallas_call(
        weight_kernel,
        grid=(width // tile,),
        in_specs=[
            pl.BlockSpec((peers, 1, rows, tile), lambda k: (0, k + first, 0, 0)),
            pl.BlockSpec((far.shape[0], tile), lambda k: (0, k)),
            whole(*g_own.shape),
            whole(*g_far.shape),
        ],
        out_specs=(pl.BlockSpec((tile, units), lambda k: (k, 0)),) * 2,
        out_shape=(shape((width, units), jnp.float32), shape((width, units))),
        compiler_params=params(1),
        cost_estimate=cost(8 * far.size * units, 4 * far.size),
    )(plane, far, g_own, g_far)


def wide_sum(a, b):
    return a.astype(jnp.float32) + b.astype(jnp.float32)


def on_device(hidden, weight):
    rows = hidden.shape[1]
    width = hidden.shape[2]
    samples = rows * DP
    units = weight.shape[1]
    peers = YS * XS
    quarter = peers * PAD

    w_far = swap(weight, view=1, z=1)
    w_sib = swap(weight, c=1)
    w_far_sib = swap(w_far, c=1)
    weights = (weight, w_sib, w_far, w_far_sib)

    plane = exchange(copies_of(hidden, peers), "yx")
    plane, w_far_sib = lax.optimization_barrier((plane, w_far_sib))

    mine = embed(plane, weights)
    from_sib = swap(mine, c=1)
    from_far = swap(mine, z=1)
    from_far_sib = swap(from_far, c=1)
    partner = swap(mine, view=1)

    h_left, h_right = compact(plane, rows)
    h_left, h_right, from_far_sib, _, _ = lax.optimization_barrier(
        (h_left, h_right, from_far_sib, from_far, from_sib)
    )
    h_left = swap(h_left, z=1)
    h_right = swap(h_right, z=1)

    centered, factor, gram = pl.pallas_call(
        functools.partial(center_kernel, rows, samples),
        grid=(1,),
        in_specs=[whole(quarter, 4 * units)] * 4,
        out_specs=(whole(4 * quarter, 4 * units), whole(8, 4 * units), whole(quarter, 4 * quarter)),
        out_shape=(
            shape((4 * quarter, 4 * units)),
            shape((8, 4 * units), jnp.float32),
            shape((quarter, 4 * quarter)),
        ),
        compiler_params=params(1),
        cost_estimate=cost(8 * 4 * quarter * quarter * units, 16 * quarter * units * 2),
    )(mine, from_sib, from_far, from_far_sib)

    gram = exchange(gram, "yx")
    gram = pl.pallas_call(
        total_kernel,
        grid=(1,),
        in_specs=[whole(*gram.shape)],
        out_specs=whole(*gram.shape),
        out_shape=shape(gram.shape),
        compiler_params=params(1),
        cost_estimate=cost(gram.size, 4 * gram.size),
    )(gram)
    gram, h_left, partner = lax.optimization_barrier((gram, h_left, partner))
    gram = exchange(gram, "yx")

    grad, g_own, g_far = pl.pallas_call(
        functools.partial(grad_kernel, rows, samples),
        grid=(1,),
        in_specs=[
            whole(quarter, 4 * quarter),
            whole(4 * quarter, 4 * units),
            whole(8, 4 * units),
            whole(quarter, 4 * units),
            whole(quarter, 4 * units),
        ],
        out_specs=(
            whole(quarter, 4 * units),
            whole(quarter, 2 * units),
            whole(peers * rows, 2 * units),
        ),
        out_shape=(shape((quarter, 4 * units)),)
        + (shape((quarter, 2 * units)), shape((peers * rows, 2 * units))),
        compiler_params=params(1),
        cost_estimate=cost(8 * 4 * quarter * quarter * units, 16 * quarter * units * 2),
    )(gram, centered, factor, mine, partner)
    g_far = swap(g_far, z=1)

    h_part = hidden_terms(grad, weights)
    h_part, g_far = lax.optimization_barrier((h_part, g_far))
    grad_rows = hidden_rows(exchange(h_part, "yx"), rows)

    first, theirs = weight_terms(plane, 0, h_left, g_own, g_far)
    theirs, h_right = lax.optimization_barrier((swap(theirs, c=1), h_right))
    first = rounded(first + theirs.astype(jnp.float32))
    second, theirs = weight_terms(plane, width // TILE // 2, h_right, g_own, g_far)
    second = rounded(second + swap(theirs, c=1).astype(jnp.float32))
    runs = [wide_sum(part, swap(part, view=1)) for part in (first, second)]
    grad_weight = jnp.concatenate(runs, axis=0) / jnp.sqrt(2.0 * samples)
    return (grad_rows, grad_weight)


def solution(mesh):
    return jax.shard_map(
        on_device,
        mesh=mesh,
        in_specs=(P("view", "dp", None), P(None, "dp")),
        out_specs=(P("view", "dp", None), P(None, "dp")),
        check_vma=False,
    )
```

```python
import functools

import jax
import jax.numpy as jnp
from jax import lax
from jax.experimental import pallas as pl
from jax.experimental.pallas import tpu as pltpu
from jax.sharding import PartitionSpec as P

YS, ZS, XS, CS = 4, 2, 4, 2
DP = YS * ZS * XS * CS
PAD = 16
TILE = 512
VMEM = 24 * 1024 * 1024


def place(d):
    return (d // (ZS * XS * CS), d // (XS * CS) % ZS, d // CS % XS, d % CS)


def index(y, z, x, c):
    return ((y * ZS + z) * XS + x) * CS + c


def groups(axes):
    found = {}
    for d in range(DP):
        key = tuple(p for p, name in zip(place(d), "yzxc") if name not in axes)
        found.setdefault(key, []).append(d)
    return list(found.values())


def swap(block, view=0, z=0, c=0):
    route = []
    for v in range(2):
        for d in range(DP):
            y, zd, x, cd = place(d)
            route.append((v * DP + d, (v ^ view) * DP + index(y, zd ^ z, x, cd ^ c)))
    return lax.ppermute(block, ("view", "dp"), route)


def exchange(blocks, axes):
    return lax.all_to_all(blocks, "dp", 0, 0, tiled=True, axis_index_groups=groups(axes))


def matmul(a, b, a_dim, b_dim):
    return lax.dot_general(
        a, b, (((a_dim,), (b_dim,)), ((), ())), preferred_element_type=jnp.float32
    )


def rounded(values):
    return lax.optimization_barrier(values.astype(jnp.bfloat16))


def reordered(block, order):
    return jnp.concatenate([block[:, 128 * i : 128 * i + 128] for i in order], axis=1)


def shape(dims, dtype=jnp.bfloat16):
    return jax.ShapeDtypeStruct(dims, dtype)


def params(steps):
    return pltpu.CompilerParams(
        vmem_limit_bytes=VMEM, dimension_semantics=("arbitrary",) * steps
    )


def cost(flops, size):
    return pl.CostEstimate(flops=flops, bytes_accessed=size, transcendentals=0)


def without_padding(x, rows):
    n = x.shape[0] // PAD * rows
    out = lax.broadcasted_iota(jnp.int32, (n, x.shape[0]), 0)
    source = lax.broadcasted_iota(jnp.int32, (n, x.shape[0]), 1)
    pick = out + out // rows * (PAD - rows) == source
    return matmul(jnp.where(pick, 1.0, 0.0).astype(x.dtype), x, 1, 0).astype(x.dtype)


def whole(*dims):
    return pl.BlockSpec(dims, lambda *_: (0,) * len(dims))


def columns(array_or_shape, count=1):
    peers, _, rows, tile = array_or_shape.shape
    return pl.BlockSpec((peers, count, rows, tile), lambda k: (0, k, 0, 0))


def joined(ref):
    n = ref.shape[0] * ref.shape[2]
    blocks = [ref[:, k].reshape(n, ref.shape[3]) for k in range(ref.shape[1])]
    return blocks[0] if len(blocks) == 1 else jnp.concatenate(blocks, axis=1)


def compact_kernel(rows, x_ref, *o_refs):
    k = 0
    for ref in o_refs:
        for at in range(0, ref.shape[1], TILE):
            block = x_ref[:, k].reshape(x_ref.shape[0] * x_ref.shape[2], TILE)
            ref[:, at : at + TILE] = without_padding(block, rows)
            k += 1


def compact(plane, rows, counts):
    peers = plane.shape[0]
    out = tuple(shape((peers * rows, count * TILE)) for count in counts)
    return pl.pallas_call(
        functools.partial(compact_kernel, rows),
        grid=(1,),
        in_specs=[whole(*plane.shape)],
        out_specs=tuple(whole(*each.shape) for each in out),
        out_shape=out,
        compiler_params=params(1),
        cost_estimate=cost(4 * plane.size, 4 * plane.size),
    )(plane)


def copies_kernel(x_ref, o_ref):
    x = x_ref[0]
    zeros = jnp.zeros((PAD - x.shape[0], x.shape[1]), x.dtype)
    x = jnp.concatenate([x, zeros], axis=0)
    for k in range(o_ref.shape[1]):
        block = x[:, TILE * k : TILE * k + TILE]
        for i in range(o_ref.shape[0]):
            o_ref[i, k] = block


def embed_kernel(h_ref, a_ref, b_ref, c_ref, d_ref, o_ref, acc_ref):
    step = pl.program_id(0)

    @pl.when(step == 0)
    def _():
        acc_ref[...] = jnp.zeros_like(acc_ref)

    w = jnp.concatenate([a_ref[...], b_ref[...], c_ref[...], d_ref[...]], axis=1)
    acc_ref[...] += matmul(joined(h_ref), w, 1, 0)

    @pl.when(step == pl.num_programs(0) - 1)
    def _():
        o_ref[...] = acc_ref[...].astype(o_ref.dtype)


def center_kernel(rows, samples, own_ref, sib_ref, far_ref, far_sib_ref, c_ref, f_ref, g_ref):
    quarter = own_ref.shape[0]
    blocks = [
        own_ref[...],
        reordered(sib_ref[...], (1, 0, 3, 2)),
        reordered(far_ref[...], (2, 3, 0, 1)),
        reordered(far_sib_ref[...], (3, 2, 1, 0)),
    ]
    wide = [block.astype(jnp.float32) for block in blocks]
    total = wide[0] + wide[1] + wide[2] + wide[3]
    mean = jnp.sum(total, axis=0, keepdims=True) * (1.0 / samples)
    real = lax.broadcasted_iota(jnp.int32, wide[0].shape, 0) % PAD < rows
    squares = jnp.zeros_like(total)
    for i, block in enumerate(wide):
        centered = jnp.where(real, block - mean, 0.0).astype(jnp.bfloat16)
        c_ref[quarter * i : quarter * i + quarter, :] = centered
        centered = centered.astype(jnp.float32)
        squares += centered * centered
    sum_squares = jnp.sum(squares, axis=0, keepdims=True)
    spread_std = jnp.sqrt(sum_squares * (1.0 / (samples - 1)) + 0.0001)
    coef_var = samples / (2.0 * (samples - 1))
    hinge = jax.nn.sigmoid(10.0 * (1.0 - spread_std))
    coef_cov = 0.08 * samples / ((samples - 1) * (samples - 1))
    factor = coef_var * hinge / spread_std + coef_cov * sum_squares
    f_ref[...] = jnp.broadcast_to(factor, f_ref.shape)
    g_ref[...] = matmul(c_ref[:quarter, :], c_ref[...], 1, 1).astype(g_ref.dtype)


def total_kernel(x_ref, o_ref):
    x = x_ref[...].reshape(x_ref.shape[0] // PAD, PAD, x_ref.shape[1])
    total = jnp.sum(x.astype(jnp.float32), axis=0).astype(o_ref.dtype)
    for i in range(o_ref.shape[0] // PAD):
        o_ref[PAD * i : PAD * i + PAD, :] = total


def grad_kernel(rows, samples, m_ref, c_ref, f_ref, e_ref, p_ref, o_ref, *run_refs):
    coef_cov = 0.08 * samples / ((samples - 1) * (samples - 1))
    coupled = matmul(m_ref[...], c_ref[...], 1, 0)
    centered = c_ref[: e_ref.shape[0], :].astype(jnp.float32)
    apart = e_ref[...].astype(jnp.float32) - p_ref[...].astype(jnp.float32)
    grad = apart - f_ref[:1, :] * centered + coef_cov * coupled
    grad = grad.astype(jnp.bfloat16)
    o_ref[...] = grad
    packed = without_padding(grad[:, 256:], rows)
    for i, ref in enumerate(run_refs[:2]):
        ref[...] = grad[:, 128 * i : 128 * i + 128]
    for i, ref in enumerate(run_refs[2:]):
        ref[...] = packed[:, 128 * i : 128 * i + 128]


def hidden_kernel(g_ref, a_ref, b_ref, c_ref, d_ref, o_ref):
    w = jnp.concatenate([a_ref[...], b_ref[...], c_ref[...], d_ref[...]], axis=1)
    out = matmul(g_ref[...], w, 1, 1).astype(o_ref.dtype)
    peers, count, rows, tile = o_ref.shape
    for k in range(count):
        o_ref[:, k] = out[:, tile * k : tile * k + tile].reshape(peers, rows, tile)


def weight_kernel(starts, *refs):
    own_ref, sib_ref, *refs = refs
    count = len(starts)
    grads, o_ref = refs[2 * count : -1], refs[-1]
    parts = [joined(own_ref), joined(sib_ref)]
    for chunks in (refs[:count], refs[count : 2 * count]):
        far = chunks[0][...]
        for start, ref in zip(starts[1:], chunks[1:]):
            far = jnp.where(pl.program_id(0) >= start, ref[...], far)
        parts.append(far)
    g = jnp.concatenate([ref[...] for ref in grads], axis=0)
    o_ref[...] = matmul(jnp.concatenate(parts, axis=0), g, 0, 0).astype(o_ref.dtype)


def rows_kernel(x_ref, o_ref):
    total = jnp.sum(x_ref[:, 0].astype(jnp.float32), axis=0)
    o_ref[0] = total[: o_ref.shape[1]]


def copies_of(block, count):
    out = shape((count, block.shape[2] // TILE, PAD, TILE))
    return pl.pallas_call(
        copies_kernel,
        grid=(1,),
        in_specs=[whole(*block.shape)],
        out_specs=whole(*out.shape),
        out_shape=out,
        compiler_params=params(1),
        cost_estimate=cost(0, 2 * count * block.size),
    )(block)


def embed(plane, weights):
    width, units = weights[0].shape
    rows = plane.size // width
    return pl.pallas_call(
        embed_kernel,
        grid=(width // TILE // 4,),
        in_specs=[columns(plane, 4)]
        + [pl.BlockSpec((4 * TILE, units), lambda k: (k, 0))] * 4,
        out_specs=whole(rows, 4 * units),
        out_shape=shape((rows, 4 * units)),
        scratch_shapes=[pltpu.VMEM((rows, 4 * units), jnp.float32)],
        compiler_params=params(1),
        cost_estimate=cost(8 * rows * width * units, 2 * width * (rows + 4 * units)),
    )(plane, *weights)


def hidden_terms(grad, weights):
    rows = grad.shape[0]
    width, units = weights[0].shape
    out = shape((rows // PAD, width // TILE, PAD, TILE))
    return pl.pallas_call(
        hidden_kernel,
        grid=(width // TILE // 4,),
        in_specs=[whole(*grad.shape)]
        + [pl.BlockSpec((4 * TILE, units), lambda k: (k, 0))] * 4,
        out_specs=columns(out, 4),
        out_shape=out,
        compiler_params=params(1),
        cost_estimate=cost(8 * rows * width * units, 2 * width * (rows + 4 * units)),
    )(grad, *weights)


def hidden_rows(pieces, rows):
    peers, blocks, _, tile = pieces.shape
    return pl.pallas_call(
        rows_kernel,
        grid=(blocks,),
        in_specs=[columns(pieces)],
        out_specs=pl.BlockSpec((1, rows, tile), lambda k: (0, 0, k)),
        out_shape=shape((1, rows, blocks * tile), jnp.float32),
        compiler_params=params(1),
        cost_estimate=cost(pieces.size, 3 * pieces.size),
    )(pieces)


def weight_terms(plane, plane_sib, first, fars, far_sibs, grads):
    peers, _, rows, tile = plane.shape
    units = grads[0].shape[1]
    starts, specs, blocks = [], [], 0
    for far in fars:
        count = far.shape[1] // tile
        starts.append(blocks)
        specs.append(
            pl.BlockSpec(
                (far.shape[0], tile),
                lambda k, start=blocks, last=count - 1: (0, jnp.clip(k - start, 0, last)),
            )
        )
        blocks += count
    width = blocks * tile
    own = pl.BlockSpec((peers, 1, rows, tile), lambda k: (0, k + first, 0, 0))
    return pl.pallas_call(
        functools.partial(weight_kernel, starts),
        grid=(blocks,),
        in_specs=[own, own] + specs + specs + [whole(*g.shape) for g in grads],
        out_specs=pl.BlockSpec((tile, units), lambda k: (k, 0)),
        out_shape=shape((width, units)),
        compiler_params=params(1),
        cost_estimate=cost(8 * peers * rows * width * units, 8 * peers * rows * width),
    )(plane, plane_sib, *fars, *far_sibs, *grads)


def wide_sum(a, b):
    return a.astype(jnp.float32) + b.astype(jnp.float32)


def on_device(hidden, weight):
    rows = hidden.shape[1]
    width = hidden.shape[2]
    samples = rows * DP
    units = weight.shape[1]
    peers = YS * XS
    quarter = peers * PAD

    w_far = swap(weight, view=1, z=1)
    w_sib = swap(weight, c=1)
    w_far_sib = swap(w_far, c=1)
    weights = (weight, w_sib, w_far, w_far_sib)

    plane = exchange(copies_of(hidden, peers), "yx")
    plane, w_far_sib = lax.optimization_barrier((plane, w_far_sib))

    mine = embed(plane, weights)
    from_sib = swap(mine, c=1)
    from_far = swap(mine, z=1)
    from_far, *h_far = lax.optimization_barrier((from_far, *compact(plane, rows, (4, 3, 1))))
    from_far_sib = swap(from_far, c=1)
    partner = swap(mine, view=1)

    h_far[0] = swap(h_far[0], z=1)
    h_far[1] = swap(h_far[1], z=1)

    centered, factor, gram = pl.pallas_call(
        functools.partial(center_kernel, rows, samples),
        grid=(1,),
        in_specs=[whole(quarter, 4 * units)] * 4,
        out_specs=(whole(4 * quarter, 4 * units), whole(8, 4 * units), whole(quarter, 4 * quarter)),
        out_shape=(
            shape((4 * quarter, 4 * units)),
            shape((8, 4 * units), jnp.float32),
            shape((quarter, 4 * quarter)),
        ),
        compiler_params=params(1),
        cost_estimate=cost(8 * 4 * quarter * quarter * units, 16 * quarter * units * 2),
    )(mine, from_sib, from_far, from_far_sib)

    gram = exchange(gram, "yx")
    gram = pl.pallas_call(
        total_kernel,
        grid=(1,),
        in_specs=[whole(*gram.shape)],
        out_specs=whole(*gram.shape),
        out_shape=shape(gram.shape),
        compiler_params=params(1),
        cost_estimate=cost(gram.size, 4 * gram.size),
    )(gram)
    gram, h_far[0], partner, plane_late = lax.optimization_barrier(
        (gram, h_far[0], partner, plane)
    )
    plane_sib = swap(plane_late, c=1)
    gram = exchange(gram, "yx")
    gram, h_far[1] = lax.optimization_barrier((gram, h_far[1]))

    grad, *runs = pl.pallas_call(
        functools.partial(grad_kernel, rows, samples),
        grid=(1,),
        in_specs=[
            whole(quarter, 4 * quarter),
            whole(4 * quarter, 4 * units),
            whole(8, 4 * units),
            whole(quarter, 4 * units),
            whole(quarter, 4 * units),
        ],
        out_specs=(whole(quarter, 4 * units),)
        + (whole(quarter, units),) * 2
        + (whole(peers * rows, units),) * 2,
        out_shape=(shape((quarter, 4 * units)),)
        + (shape((quarter, units)),) * 2
        + (shape((peers * rows, units)),) * 2,
        compiler_params=params(1),
        cost_estimate=cost(8 * 4 * quarter * quarter * units, 16 * quarter * units * 2),
    )(gram, centered, factor, mine, partner)
    g_far = swap(runs[2], z=1)
    g_far_sib = swap(runs[3], z=1, c=1)
    g_sib = swap(runs[1], c=1)
    h_part = hidden_terms(grad, weights)
    h_part, *grads = lax.optimization_barrier((h_part, runs[0], g_sib, g_far, g_far_sib))
    h_far[2], *grads = lax.optimization_barrier((h_far[2], *grads))
    h_far[2] = swap(h_far[2], z=1)

    grad_rows = hidden_rows(exchange(h_part, "yx"), rows)

    far_sibs = [swap(block, c=1) for block in h_far]
    runs = []
    for first, which in ((0, slice(0, 2)), (7, slice(2, 3))):
        part = weight_terms(plane, plane_sib, first, h_far[which], far_sibs[which], grads)
        runs.append(wide_sum(part, swap(part, view=1)))
    grad_weight = jnp.concatenate(runs, axis=0) / jnp.sqrt(2.0 * samples)
    return (grad_rows, grad_weight)


def solution(mesh):
    return jax.shard_map(
        on_device,
        mesh=mesh,
        in_specs=(P("view", "dp", None), P(None, "dp")),
        out_specs=(P("view", "dp", None), P(None, "dp")),
        check_vma=False,
    )
```

```python
import functools

import jax
import jax.numpy as jnp
from jax import lax
from jax.experimental import pallas as pl
from jax.experimental.pallas import tpu as pltpu
from jax.sharding import PartitionSpec as P

YS, ZS, XS, CS = 4, 2, 4, 2
DP = YS * ZS * XS * CS
PAD = 16
TILE = 1024
VMEM = 24 * 1024 * 1024


def place(d):
    return (d // (ZS * XS * CS), d // (XS * CS) % ZS, d // CS % XS, d % CS)


def index(y, z, x, c):
    return ((y * ZS + z) * XS + x) * CS + c


def groups(axes):
    found = {}
    for d in range(DP):
        key = tuple(p for p, name in zip(place(d), "yzxc") if name not in axes)
        found.setdefault(key, []).append(d)
    return list(found.values())


def swap(block, view=0, z=0, c=0):
    route = []
    for v in range(2):
        for d in range(DP):
            y, zd, x, cd = place(d)
            route.append((v * DP + d, (v ^ view) * DP + index(y, zd ^ z, x, cd ^ c)))
    return lax.ppermute(block, ("view", "dp"), route)


def exchange(blocks, axes):
    return lax.all_to_all(blocks, "dp", 0, 0, tiled=True, axis_index_groups=groups(axes))


def matmul(a, b, a_dim, b_dim):
    return lax.dot_general(
        a, b, (((a_dim,), (b_dim,)), ((), ())), preferred_element_type=jnp.float32
    )


def rounded(values):
    return lax.optimization_barrier(values.astype(jnp.bfloat16))


def reordered(block, order):
    return jnp.concatenate([block[:, 128 * i : 128 * i + 128] for i in order], axis=1)


def shape(dims, dtype=jnp.bfloat16):
    return jax.ShapeDtypeStruct(dims, dtype)


def params(steps):
    return pltpu.CompilerParams(
        vmem_limit_bytes=VMEM, dimension_semantics=("arbitrary",) * steps
    )


def cost(flops, size):
    return pl.CostEstimate(flops=flops, bytes_accessed=size, transcendentals=0)


def without_padding(x, rows):
    n = x.shape[0] // PAD * rows
    out = lax.broadcasted_iota(jnp.int32, (n, x.shape[0]), 0)
    source = lax.broadcasted_iota(jnp.int32, (n, x.shape[0]), 1)
    pick = out + out // rows * (PAD - rows) == source
    return matmul(jnp.where(pick, 1.0, 0.0).astype(x.dtype), x, 1, 0).astype(x.dtype)


def whole(*dims):
    return pl.BlockSpec(dims, lambda *_: (0,) * len(dims))


def columns(array_or_shape, count=1):
    peers, _, rows, tile = array_or_shape.shape
    return pl.BlockSpec((peers, count, rows, tile), lambda k: (0, k, 0, 0))


def joined(ref):
    n = ref.shape[0] * ref.shape[2]
    blocks = [ref[:, k].reshape(n, ref.shape[3]) for k in range(ref.shape[1])]
    return blocks[0] if len(blocks) == 1 else jnp.concatenate(blocks, axis=1)


def compact_kernel(rows, x_ref, o_ref):
    o_ref[...] = without_padding(joined(x_ref), rows)


def compact(plane, rows):
    peers, blocks, _, tile = plane.shape
    return pl.pallas_call(
        functools.partial(compact_kernel, rows),
        grid=(blocks // 2,),
        in_specs=[columns(plane, 2)],
        out_specs=pl.BlockSpec((peers * rows, 2 * tile), lambda k: (0, k)),
        out_shape=shape((peers * rows, blocks * tile)),
        compiler_params=params(1),
        cost_estimate=cost(4 * plane.size, 4 * plane.size),
    )(plane)


def copies_kernel(x_ref, o_ref):
    x = x_ref[0]
    zeros = jnp.zeros((PAD - x.shape[0], x.shape[1]), x.dtype)
    x = jnp.concatenate([x, zeros], axis=0)
    for k in range(o_ref.shape[1]):
        block = x[:, TILE * k : TILE * k + TILE]
        for i in range(o_ref.shape[0]):
            o_ref[i, k] = block


def embed_kernel(h_ref, a_ref, b_ref, c_ref, d_ref, o_ref, acc_ref):
    step = pl.program_id(0)

    @pl.when(step == 0)
    def _():
        acc_ref[...] = jnp.zeros_like(acc_ref)

    w = jnp.concatenate([a_ref[...], b_ref[...], c_ref[...], d_ref[...]], axis=1)
    acc_ref[...] += matmul(joined(h_ref), w, 1, 0)

    @pl.when(step == pl.num_programs(0) - 1)
    def _():
        o_ref[...] = acc_ref[...].astype(o_ref.dtype)


def center_kernel(rows, samples, own_ref, sib_ref, far_ref, far_sib_ref, c_ref, f_ref, g_ref):
    quarter = own_ref.shape[0]
    blocks = [
        own_ref[...],
        reordered(sib_ref[...], (1, 0, 3, 2)),
        reordered(far_ref[...], (2, 3, 0, 1)),
        reordered(far_sib_ref[...], (3, 2, 1, 0)),
    ]
    wide = [block.astype(jnp.float32) for block in blocks]
    total = wide[0] + wide[1] + wide[2] + wide[3]
    mean = jnp.sum(total, axis=0, keepdims=True) * (1.0 / samples)
    real = lax.broadcasted_iota(jnp.int32, wide[0].shape, 0) % PAD < rows
    squares = jnp.zeros_like(total)
    for i, block in enumerate(wide):
        centered = jnp.where(real, block - mean, 0.0).astype(jnp.bfloat16)
        c_ref[quarter * i : quarter * i + quarter, :] = centered
        centered = centered.astype(jnp.float32)
        squares += centered * centered
    sum_squares = jnp.sum(squares, axis=0, keepdims=True)
    spread_std = jnp.sqrt(sum_squares * (1.0 / (samples - 1)) + 0.0001)
    coef_var = samples / (2.0 * (samples - 1))
    hinge = jax.nn.sigmoid(10.0 * (1.0 - spread_std))
    coef_cov = 0.08 * samples / ((samples - 1) * (samples - 1))
    factor = coef_var * hinge / spread_std + coef_cov * sum_squares
    f_ref[...] = jnp.broadcast_to(factor, f_ref.shape)
    g_ref[...] = matmul(c_ref[:quarter, :], c_ref[...], 1, 1).astype(g_ref.dtype)


def total_kernel(x_ref, o_ref):
    x = x_ref[...].reshape(x_ref.shape[0] // PAD, PAD, x_ref.shape[1])
    total = jnp.sum(x.astype(jnp.float32), axis=0).astype(o_ref.dtype)
    for i in range(o_ref.shape[0] // PAD):
        o_ref[PAD * i : PAD * i + PAD, :] = total


def grad_kernel(rows, samples, m_ref, c_ref, f_ref, e_ref, p_ref, o_ref, *run_refs):
    coef_cov = 0.08 * samples / ((samples - 1) * (samples - 1))
    coupled = matmul(m_ref[...], c_ref[...], 1, 0)
    centered = c_ref[: e_ref.shape[0], :].astype(jnp.float32)
    apart = e_ref[...].astype(jnp.float32) - p_ref[...].astype(jnp.float32)
    grad = apart - f_ref[:1, :] * centered + coef_cov * coupled
    grad = grad.astype(jnp.bfloat16)
    o_ref[...] = grad
    packed = without_padding(grad, rows)
    for i, ref in enumerate(run_refs):
        ref[...] = packed[:, 128 * i : 128 * i + 128]


def hidden_kernel(g_ref, a_ref, b_ref, c_ref, d_ref, o_ref):
    w = jnp.concatenate([a_ref[...], b_ref[...], c_ref[...], d_ref[...]], axis=1)
    out = matmul(g_ref[...], w, 1, 1).astype(o_ref.dtype)
    peers, count, rows, tile = o_ref.shape
    for k in range(count):
        o_ref[:, k] = out[:, tile * k : tile * k + tile].reshape(peers, rows, tile)


def weight_kernel(z_ref, own_ref, sib_ref, *refs):
    near, near_sib, far, far_sib, o_ref = refs
    n = own_ref.shape[1]
    h = [ref[i] for ref in (own_ref, sib_ref) for i in range(2)]
    first = z_ref[0] == 0
    g = []
    for a, b in ((near[...], far[...]), (near_sib[...], far_sib[...])):
        g += [jnp.where(first, a, b), jnp.where(first, b, a)]
    o_ref[...] = matmul(jnp.concatenate(h, axis=0), jnp.concatenate(g, axis=0), 0, 0).astype(
        o_ref.dtype
    )


def rows_kernel(x_ref, o_ref):
    total = jnp.sum(x_ref[:, 0].astype(jnp.float32), axis=0)
    o_ref[0] = total[: o_ref.shape[1]]


def copies_of(block, count):
    out = shape((count, block.shape[2] // TILE, PAD, TILE))
    return pl.pallas_call(
        copies_kernel,
        grid=(1,),
        in_specs=[whole(*block.shape)],
        out_specs=whole(*out.shape),
        out_shape=out,
        compiler_params=params(1),
        cost_estimate=cost(0, 2 * count * block.size),
    )(block)


def embed(plane, weights):
    width, units = weights[0].shape
    rows = plane.size // width
    return pl.pallas_call(
        embed_kernel,
        grid=(width // TILE // 2,),
        in_specs=[columns(plane, 2)]
        + [pl.BlockSpec((2 * TILE, units), lambda k: (k, 0))] * 4,
        out_specs=whole(rows, 4 * units),
        out_shape=shape((rows, 4 * units)),
        scratch_shapes=[pltpu.VMEM((rows, 4 * units), jnp.float32)],
        compiler_params=params(1),
        cost_estimate=cost(8 * rows * width * units, 2 * width * (rows + 4 * units)),
    )(plane, *weights)


def hidden_terms(grad, weights):
    rows = grad.shape[0]
    width, units = weights[0].shape
    out = shape((rows // PAD, width // TILE, PAD, TILE))
    return pl.pallas_call(
        hidden_kernel,
        grid=(width // TILE // 2,),
        in_specs=[whole(*grad.shape)]
        + [pl.BlockSpec((2 * TILE, units), lambda k: (k, 0))] * 4,
        out_specs=columns(out, 2),
        out_shape=out,
        compiler_params=params(1),
        cost_estimate=cost(8 * rows * width * units, 2 * width * (rows + 4 * units)),
    )(grad, *weights)


def hidden_rows(pieces, rows):
    peers, blocks, _, tile = pieces.shape
    return pl.pallas_call(
        rows_kernel,
        grid=(blocks,),
        in_specs=[columns(pieces)],
        out_specs=pl.BlockSpec((1, rows, tile), lambda k: (0, 0, k)),
        out_shape=shape((1, rows, blocks * tile), jnp.float32),
        compiler_params=params(1),
        cost_estimate=cost(pieces.size, 3 * pieces.size),
    )(pieces)


def weight_terms(z, both, both_sib, part, grads):
    _, rows, width = both.shape
    units = grads[0].shape[1]
    tile, count = width // 4, 2
    block = pl.BlockSpec((2, rows, tile), lambda k: (0, 0, k + count * part))
    return pl.pallas_call(
        weight_kernel,
        grid=(count,),
        in_specs=[pl.BlockSpec(memory_space=pltpu.SMEM), block, block]
        + [whole(*g.shape) for g in grads],
        out_specs=pl.BlockSpec((tile, units), lambda k: (k, 0)),
        out_shape=shape((width // 2, units)),
        compiler_params=params(1),
        cost_estimate=cost(4 * rows * width * units, 4 * rows * width),
    )(z, both, both_sib, *grads)


def wide_sum(a, b):
    return a.astype(jnp.float32) + b.astype(jnp.float32)


def on_device(hidden, weight):
    rows = hidden.shape[1]
    width = hidden.shape[2]
    samples = rows * DP
    units = weight.shape[1]
    peers = YS * XS
    quarter = peers * PAD

    w_far = swap(weight, view=1, z=1)
    w_sib = swap(weight, c=1)
    w_far_sib = swap(w_far, c=1)
    weights = (weight, w_sib, w_far, w_far_sib)

    plane = exchange(copies_of(hidden, peers), "yx")
    plane, w_far_sib = lax.optimization_barrier((plane, w_far_sib))

    mine = embed(plane, weights)
    from_sib = swap(mine, c=1)
    from_far = swap(mine, z=1)
    from_far, packed = lax.optimization_barrier((from_far, compact(plane, rows)))
    both = lax.all_gather(packed, "dp", axis_index_groups=groups("z"))
    from_far_sib = swap(from_far, c=1)
    partner = swap(mine, view=1)

    centered, factor, gram = pl.pallas_call(
        functools.partial(center_kernel, rows, samples),
        grid=(1,),
        in_specs=[whole(quarter, 4 * units)] * 4,
        out_specs=(whole(4 * quarter, 4 * units), whole(8, 4 * units), whole(quarter, 4 * quarter)),
        out_shape=(
            shape((4 * quarter, 4 * units)),
            shape((8, 4 * units), jnp.float32),
            shape((quarter, 4 * quarter)),
        ),
        compiler_params=params(1),
        cost_estimate=cost(8 * 4 * quarter * quarter * units, 16 * quarter * units * 2),
    )(mine, from_sib, from_far, from_far_sib)

    gram = exchange(gram, "yx")
    gram = pl.pallas_call(
        total_kernel,
        grid=(1,),
        in_specs=[whole(*gram.shape)],
        out_specs=whole(*gram.shape),
        out_shape=shape(gram.shape),
        compiler_params=params(1),
        cost_estimate=cost(gram.size, 4 * gram.size),
    )(gram)
    gram, partner = lax.optimization_barrier((gram, partner))
    gram = exchange(gram, "yx")

    grad, *runs = pl.pallas_call(
        functools.partial(grad_kernel, rows, samples),
        grid=(1,),
        in_specs=[
            whole(quarter, 4 * quarter),
            whole(4 * quarter, 4 * units),
            whole(8, 4 * units),
            whole(quarter, 4 * units),
            whole(quarter, 4 * units),
        ],
        out_specs=(whole(quarter, 4 * units),)
        + (whole(peers * rows, units),) * 4,
        out_shape=(shape((quarter, 4 * units)),)
        + (shape((peers * rows, units)),) * 4,
        compiler_params=params(1),
        cost_estimate=cost(8 * 4 * quarter * quarter * units, 16 * quarter * units * 2),
    )(gram, centered, factor, mine, partner)
    g_far = swap(runs[2], z=1)
    g_far_sib = swap(runs[3], z=1, c=1)
    g_sib = swap(runs[1], c=1)
    h_part = hidden_terms(grad, weights)
    h_part, both, *grads = lax.optimization_barrier(
        (h_part, both, runs[0], g_sib, g_far, g_far_sib)
    )

    grad_rows = hidden_rows(exchange(h_part, "yx"), rows)

    both_sib = swap(both, c=1)
    z = (lax.axis_index("dp") // (XS * CS) % ZS).astype(jnp.int32).reshape(1)
    parts = [weight_terms(z, both, both_sib, part, grads) for part in (0, 1)]
    runs = [wide_sum(part, swap(part, view=1)) for part in parts]
    grad_weight = jnp.concatenate(runs, axis=0) / jnp.sqrt(2.0 * samples)
    return (grad_rows, grad_weight)


def solution(mesh):
    return jax.shard_map(
        on_device,
        mesh=mesh,
        in_specs=(P("view", "dp", None), P(None, "dp")),
        out_specs=(P("view", "dp", None), P(None, "dp")),
        check_vma=False,
    )
```

```python
import functools
import math

import jax
import jax.numpy as jnp
from jax import lax
from jax.experimental import pallas as pl
from jax.experimental.pallas import tpu as pltpu
from jax.sharding import PartitionSpec as P

YS, ZS, XS, CS = 4, 2, 4, 2
DP = YS * ZS * XS * CS
PAD = 16
TILE = 512
VMEM = 24 * 1024 * 1024


def place(d):
    return (d // (ZS * XS * CS), d // (XS * CS) % ZS, d // CS % XS, d % CS)


def index(y, z, x, c):
    return ((y * ZS + z) * XS + x) * CS + c


def groups(axes):
    found = {}
    for d in range(DP):
        key = tuple(p for p, name in zip(place(d), "yzxc") if name not in axes)
        found.setdefault(key, []).append(d)
    return list(found.values())


def swap(block, view=0, z=0, c=0):
    route = []
    for v in range(2):
        for d in range(DP):
            y, zd, x, cd = place(d)
            route.append((v * DP + d, (v ^ view) * DP + index(y, zd ^ z, x, cd ^ c)))
    return lax.ppermute(block, ("view", "dp"), route)


def exchange(blocks, axes):
    return lax.all_to_all(blocks, "dp", 0, 0, tiled=True, axis_index_groups=groups(axes))


def matmul(a, b, a_dim, b_dim):
    return lax.dot_general(
        a, b, (((a_dim,), (b_dim,)), ((), ())), preferred_element_type=jnp.float32
    )


def rounded(values):
    return lax.optimization_barrier(values.astype(jnp.bfloat16))


def reordered(block, order):
    return jnp.concatenate([block[:, 128 * i : 128 * i + 128] for i in order], axis=1)


def shape(dims, dtype=jnp.bfloat16):
    return jax.ShapeDtypeStruct(dims, dtype)


def params(steps):
    return pltpu.CompilerParams(
        vmem_limit_bytes=VMEM, dimension_semantics=("arbitrary",) * steps
    )


def cost(flops, size):
    return pl.CostEstimate(flops=flops, bytes_accessed=size, transcendentals=0)


def without_padding(x, rows):
    n = x.shape[0] // PAD * rows
    out = lax.broadcasted_iota(jnp.int32, (n, x.shape[0]), 0)
    source = lax.broadcasted_iota(jnp.int32, (n, x.shape[0]), 1)
    pick = out + out // rows * (PAD - rows) == source
    return matmul(jnp.where(pick, 1.0, 0.0).astype(x.dtype), x, 1, 0).astype(x.dtype)


def whole(*dims):
    return pl.BlockSpec(dims, lambda *_: (0,) * len(dims))


def columns(array_or_shape, count=1):
    peers, _, rows, tile = array_or_shape.shape
    return pl.BlockSpec((peers, count, rows, tile), lambda k: (0, k, 0, 0))


def joined(ref):
    n = ref.shape[0] * ref.shape[2]
    blocks = [ref[:, k].reshape(n, ref.shape[3]) for k in range(ref.shape[1])]
    return blocks[0] if len(blocks) == 1 else jnp.concatenate(blocks, axis=1)


def compact_kernel(rows, x_ref, *o_refs):
    at = 0
    for ref in o_refs:
        blocks = ref.shape[1] // TILE
        ref[...] = without_padding(joined(x_ref.at[:, at : at + blocks]), rows)
        at += blocks


def compact(plane, rows, widths):
    peers = plane.shape[0]
    out = tuple(shape((peers * rows, width)) for width in widths)
    return pl.pallas_call(
        functools.partial(compact_kernel, rows),
        grid=(1,),
        in_specs=[whole(*plane.shape)],
        out_specs=tuple(whole(*each.shape) for each in out),
        out_shape=out,
        compiler_params=params(1),
        cost_estimate=cost(4 * plane.size, 4 * plane.size),
    )(plane)


def copies_kernel(x_ref, o_ref):
    x = x_ref[0]
    zeros = jnp.zeros((PAD - x.shape[0], x.shape[1]), x.dtype)
    x = jnp.concatenate([x, zeros], axis=0)
    for k in range(o_ref.shape[1]):
        block = x[:, TILE * k : TILE * k + TILE]
        for i in range(o_ref.shape[0]):
            o_ref[i, k] = block


def embed_kernel(h_ref, a_ref, b_ref, c_ref, d_ref, o_ref, acc_ref):
    step = pl.program_id(0)

    @pl.when(step == 0)
    def _():
        acc_ref[...] = jnp.zeros_like(acc_ref)

    w = jnp.concatenate([a_ref[...], b_ref[...], c_ref[...], d_ref[...]], axis=1)
    acc_ref[...] += matmul(joined(h_ref), w, 1, 0)

    @pl.when(step == pl.num_programs(0) - 1)
    def _():
        o_ref[...] = acc_ref[...].astype(o_ref.dtype)


def center_kernel(rows, samples, own_ref, sib_ref, far_ref, far_sib_ref, c_ref, f_ref, g_ref):
    quarter = own_ref.shape[0]
    blocks = [
        own_ref[...],
        reordered(sib_ref[...], (1, 0, 3, 2)),
        reordered(far_ref[...], (2, 3, 0, 1)),
        reordered(far_sib_ref[...], (3, 2, 1, 0)),
    ]
    wide = [block.astype(jnp.float32) for block in blocks]
    total = wide[0] + wide[1] + wide[2] + wide[3]
    mean = jnp.sum(total, axis=0, keepdims=True) * (1.0 / samples)
    real = lax.broadcasted_iota(jnp.int32, wide[0].shape, 0) % PAD < rows
    squares = jnp.zeros_like(total)
    for i, block in enumerate(wide):
        centered = jnp.where(real, block - mean, 0.0).astype(jnp.bfloat16)
        c_ref[quarter * i : quarter * i + quarter, :] = centered
        centered = centered.astype(jnp.float32)
        squares += centered * centered
    sum_squares = jnp.sum(squares, axis=0, keepdims=True)
    spread_std = jnp.sqrt(sum_squares * (1.0 / (samples - 1)) + 0.0001)
    coef_var = samples / (2.0 * (samples - 1))
    hinge = jax.nn.sigmoid(10.0 * (1.0 - spread_std))
    coef_cov = 0.08 * samples / ((samples - 1) * (samples - 1))
    factor = coef_var * hinge / spread_std + coef_cov * sum_squares
    f_ref[...] = jnp.broadcast_to(factor, f_ref.shape)
    g_ref[...] = matmul(c_ref[:quarter, :], c_ref[...], 1, 1).astype(g_ref.dtype)


def total_kernel(x_ref, o_ref):
    x = x_ref[...].reshape(x_ref.shape[0] // PAD, PAD, x_ref.shape[1])
    total = jnp.sum(x.astype(jnp.float32), axis=0).astype(o_ref.dtype)
    for i in range(o_ref.shape[0] // PAD):
        o_ref[PAD * i : PAD * i + PAD, :] = total


def grad_kernel(rows, samples, m_ref, c_ref, f_ref, e_ref, p_ref, o_ref, *run_refs):
    coef_cov = 0.08 * samples / ((samples - 1) * (samples - 1))
    coupled = matmul(m_ref[...], c_ref[...], 1, 0)
    centered = c_ref[: e_ref.shape[0], :].astype(jnp.float32)
    apart = e_ref[...].astype(jnp.float32) - p_ref[...].astype(jnp.float32)
    grad = apart - f_ref[:1, :] * centered + coef_cov * coupled
    grad = grad.astype(jnp.bfloat16)
    o_ref[...] = grad
    packed = without_padding(grad, rows)
    for i, ref in enumerate(run_refs):
        ref[...] = packed[:, 128 * i : 128 * i + 128]


def hidden_kernel(g_ref, a_ref, b_ref, c_ref, d_ref, o_ref):
    w = jnp.concatenate([a_ref[...], b_ref[...], c_ref[...], d_ref[...]], axis=1)
    out = matmul(g_ref[...], w, 1, 1).astype(o_ref.dtype)
    peers, count, rows, tile = o_ref.shape
    for k in range(count):
        o_ref[:, k] = out[:, tile * k : tile * k + tile].reshape(peers, rows, tile)


def weight_kernel(*refs):
    hs, gs, (o_ref,) = refs[:4], refs[4:8], refs[8:]
    h = jnp.concatenate([ref[...] for ref in hs], axis=0)
    g = jnp.concatenate([ref[...] for ref in gs], axis=0)
    o_ref[...] = matmul(h, g, 0, 0).astype(o_ref.dtype)


def ends_kernel(scale, *refs):
    pairs, (o_ref,) = refs[:-1], refs[-1:]
    at = 0
    for a_ref, b_ref in zip(pairs[::2], pairs[1::2]):
        n = a_ref.shape[0]
        total = a_ref[...].astype(jnp.float32) + b_ref[...].astype(jnp.float32)
        o_ref[at : at + n, :] = total / scale
        at += n


def rows_kernel(x_ref, o_ref):
    total = jnp.sum(x_ref[:, 0].astype(jnp.float32), axis=0)
    o_ref[0] = total[: o_ref.shape[1]]


def copies_of(block, count):
    out = shape((count, block.shape[2] // TILE, PAD, TILE))
    return pl.pallas_call(
        copies_kernel,
        grid=(1,),
        in_specs=[whole(*block.shape)],
        out_specs=whole(*out.shape),
        out_shape=out,
        compiler_params=params(1),
        cost_estimate=cost(0, 2 * count * block.size),
    )(block)


def embed(plane, weights):
    width, units = weights[0].shape
    rows = plane.size // width
    return pl.pallas_call(
        embed_kernel,
        grid=(width // TILE // 4,),
        in_specs=[columns(plane, 4)]
        + [pl.BlockSpec((4 * TILE, units), lambda k: (k, 0))] * 4,
        out_specs=whole(rows, 4 * units),
        out_shape=shape((rows, 4 * units)),
        scratch_shapes=[pltpu.VMEM((rows, 4 * units), jnp.float32)],
        compiler_params=params(1),
        cost_estimate=cost(8 * rows * width * units, 2 * width * (rows + 4 * units)),
    )(plane, *weights)


def hidden_terms(grad, weights):
    rows = grad.shape[0]
    width, units = weights[0].shape
    out = shape((rows // PAD, width // TILE, PAD, TILE))
    return pl.pallas_call(
        hidden_kernel,
        grid=(width // TILE // 4,),
        in_specs=[whole(*grad.shape)]
        + [pl.BlockSpec((4 * TILE, units), lambda k: (k, 0))] * 4,
        out_specs=columns(out, 4),
        out_shape=out,
        compiler_params=params(1),
        cost_estimate=cost(8 * rows * width * units, 2 * width * (rows + 4 * units)),
    )(grad, *weights)


def hidden_rows(pieces, rows):
    peers, blocks, _, tile = pieces.shape
    return pl.pallas_call(
        rows_kernel,
        grid=(blocks,),
        in_specs=[columns(pieces)],
        out_specs=pl.BlockSpec((1, rows, tile), lambda k: (0, 0, k)),
        out_shape=shape((1, rows, blocks * tile), jnp.float32),
        compiler_params=params(1),
        cost_estimate=cost(pieces.size, 3 * pieces.size),
    )(pieces)


def weight_terms(parts, grads):
    rows, width = parts[0].shape
    units = grads[0].shape[1]
    return pl.pallas_call(
        weight_kernel,
        grid=(width // TILE,),
        in_specs=[pl.BlockSpec((rows, TILE), lambda k: (0, k))] * 4
        + [whole(*g.shape) for g in grads],
        out_specs=pl.BlockSpec((TILE, units), lambda k: (k, 0)),
        out_shape=shape((width, units)),
        compiler_params=params(1),
        cost_estimate=cost(8 * rows * width * units, 8 * rows * width),
    )(*parts, *grads)


def view_sums(parts, samples):
    arrays = [each for part in parts for each in (part, swap(part, view=1))]
    total = sum(part.shape[0] for part in parts)
    units = parts[0].shape[1]
    return pl.pallas_call(
        functools.partial(ends_kernel, math.sqrt(2.0 * samples)),
        grid=(1,),
        in_specs=[whole(*each.shape) for each in arrays],
        out_specs=whole(total, units),
        out_shape=shape((total, units), jnp.float32),
        compiler_params=params(1),
        cost_estimate=cost(total * units, 8 * total * units),
    )(*arrays)


def on_device(hidden, weight):
    rows = hidden.shape[1]
    width = hidden.shape[2]
    samples = rows * DP
    units = weight.shape[1]
    peers = YS * XS
    quarter = peers * PAD

    w_far = swap(weight, view=1, z=1)
    w_sib = swap(weight, c=1)
    w_far_sib = swap(w_far, c=1)
    weights = (weight, w_sib, w_far, w_far_sib)

    plane = exchange(copies_of(hidden, peers), "yx")
    plane, w_far_sib = lax.optimization_barrier((plane, w_far_sib))

    mine = embed(plane, weights)
    from_sib = swap(mine, c=1)
    from_far = swap(mine, z=1)
    split = (3 * width // 8, 5 * width // 8)
    from_far, *h_own = lax.optimization_barrier((from_far, *compact(plane, rows, split)))
    from_far_sib = swap(from_far, c=1)
    partner = swap(mine, view=1)
    first, partner = lax.optimization_barrier((h_own[0], partner))
    h_far = [swap(first, z=1), swap(h_own[1], z=1)]

    centered, factor, gram = pl.pallas_call(
        functools.partial(center_kernel, rows, samples),
        grid=(1,),
        in_specs=[whole(quarter, 4 * units)] * 4,
        out_specs=(whole(4 * quarter, 4 * units), whole(8, 4 * units), whole(quarter, 4 * quarter)),
        out_shape=(
            shape((4 * quarter, 4 * units)),
            shape((8, 4 * units), jnp.float32),
            shape((quarter, 4 * quarter)),
        ),
        compiler_params=params(1),
        cost_estimate=cost(8 * 4 * quarter * quarter * units, 16 * quarter * units * 2),
    )(mine, from_sib, from_far, from_far_sib)

    gram = exchange(gram, "yx")
    gram = pl.pallas_call(
        total_kernel,
        grid=(1,),
        in_specs=[whole(*gram.shape)],
        out_specs=whole(*gram.shape),
        out_shape=shape(gram.shape),
        compiler_params=params(1),
        cost_estimate=cost(gram.size, 4 * gram.size),
    )(gram)
    gram, h_far[0], *late = lax.optimization_barrier((gram, h_far[0], *h_own))
    h_sib = [swap(block, c=1) for block in late]
    gram = exchange(gram, "yx")

    grad, *runs = pl.pallas_call(
        functools.partial(grad_kernel, rows, samples),
        grid=(1,),
        in_specs=[
            whole(quarter, 4 * quarter),
            whole(4 * quarter, 4 * units),
            whole(8, 4 * units),
            whole(quarter, 4 * units),
            whole(quarter, 4 * units),
        ],
        out_specs=(whole(quarter, 4 * units),)
        + (whole(peers * rows, units),) * 4,
        out_shape=(shape((quarter, 4 * units)),)
        + (shape((peers * rows, units)),) * 4,
        compiler_params=params(1),
        cost_estimate=cost(8 * 4 * quarter * quarter * units, 16 * quarter * units * 2),
    )(gram, centered, factor, mine, partner)
    g_far = swap(runs[2], z=1)
    g_far_sib = swap(runs[3], z=1, c=1)
    g_sib = swap(runs[1], c=1)
    h_part = hidden_terms(grad, weights)
    h_part, h_far[1], *grads = lax.optimization_barrier(
        (h_part, h_far[1], runs[0], g_sib, g_far, g_far_sib)
    )
    pieces = exchange(h_part, "yx")

    parts = [
        weight_terms((own, sib, far, swap(far, c=1)), grads)
        for own, sib, far in zip(h_own, h_sib, h_far)
    ]
    grad_weight, pieces = lax.optimization_barrier((view_sums(parts, samples), pieces))
    grad_rows = hidden_rows(pieces, rows)
    return (grad_rows, grad_weight)


def solution(mesh):
    return jax.shard_map(
        on_device,
        mesh=mesh,
        in_specs=(P("view", "dp", None), P(None, "dp")),
        out_specs=(P("view", "dp", None), P(None, "dp")),
        check_vma=False,
    )
```

```python
import functools
import math

import jax
import jax.numpy as jnp
from jax import lax
from jax.experimental import pallas as pl
from jax.experimental.pallas import tpu as pltpu
from jax.sharding import PartitionSpec as P

YS, ZS, XS, CS = 4, 2, 4, 2
DP = YS * ZS * XS * CS
PAD = 16
TILE = 512
VMEM = 24 * 1024 * 1024
FULL = 60 * 1024 * 1024


def place(d):
    return (d // (ZS * XS * CS), d // (XS * CS) % ZS, d // CS % XS, d % CS)


def index(y, z, x, c):
    return ((y * ZS + z) * XS + x) * CS + c


def groups(axes):
    found = {}
    for d in range(DP):
        key = tuple(p for p, name in zip(place(d), "yzxc") if name not in axes)
        found.setdefault(key, []).append(d)
    return list(found.values())


def swap(block, view=0, z=0, c=0):
    route = []
    for v in range(2):
        for d in range(DP):
            y, zd, x, cd = place(d)
            route.append((v * DP + d, (v ^ view) * DP + index(y, zd ^ z, x, cd ^ c)))
    return lax.ppermute(block, ("view", "dp"), route)


def exchange(blocks, axes):
    return lax.all_to_all(blocks, "dp", 0, 0, tiled=True, axis_index_groups=groups(axes))


def matmul(a, b, a_dim, b_dim):
    return lax.dot_general(
        a, b, (((a_dim,), (b_dim,)), ((), ())), preferred_element_type=jnp.float32
    )


def rounded(values):
    return lax.optimization_barrier(values.astype(jnp.bfloat16))


def reordered(block, order):
    return jnp.concatenate([block[:, 128 * i : 128 * i + 128] for i in order], axis=1)


def shape(dims, dtype=jnp.bfloat16):
    return jax.ShapeDtypeStruct(dims, dtype)


def params(steps, vmem=VMEM):
    return pltpu.CompilerParams(
        vmem_limit_bytes=vmem, dimension_semantics=("arbitrary",) * steps
    )


def cost(flops, size):
    return pl.CostEstimate(flops=flops, bytes_accessed=size, transcendentals=0)


def without_padding(x, rows):
    n = x.shape[0] // PAD * rows
    out = lax.broadcasted_iota(jnp.int32, (n, x.shape[0]), 0)
    source = lax.broadcasted_iota(jnp.int32, (n, x.shape[0]), 1)
    pick = out + out // rows * (PAD - rows) == source
    return matmul(jnp.where(pick, 1.0, 0.0).astype(x.dtype), x, 1, 0).astype(x.dtype)


def whole(*dims):
    return pl.BlockSpec(dims, lambda *_: (0,) * len(dims))


def columns(array_or_shape, count=1):
    peers, _, rows, tile = array_or_shape.shape
    return pl.BlockSpec((peers, count, rows, tile), lambda k: (0, k, 0, 0))


def joined(ref):
    n = ref.shape[0] * ref.shape[2]
    blocks = [ref[:, k].reshape(n, ref.shape[3]) for k in range(ref.shape[1])]
    return blocks[0] if len(blocks) == 1 else jnp.concatenate(blocks, axis=1)


def compact_kernel(rows, x_ref, all_ref, *o_refs):
    at = 0
    for ref in o_refs:
        blocks = ref.shape[1] // TILE
        packed = without_padding(joined(x_ref.at[:, at : at + blocks]), rows)
        ref[...] = packed
        all_ref[:, TILE * at : TILE * (at + blocks)] = packed
        at += blocks


def compact(plane, rows, widths):
    peers = plane.shape[0]
    out = tuple(shape((peers * rows, width)) for width in (sum(widths), *widths))
    return pl.pallas_call(
        functools.partial(compact_kernel, rows),
        grid=(1,),
        in_specs=[whole(*plane.shape)],
        out_specs=tuple(whole(*each.shape) for each in out),
        out_shape=out,
        compiler_params=params(1, FULL),
        cost_estimate=cost(4 * plane.size, 4 * plane.size),
    )(plane)


def copies_kernel(x_ref, o_ref):
    x = x_ref[0]
    zeros = jnp.zeros((PAD - x.shape[0], x.shape[1]), x.dtype)
    x = jnp.concatenate([x, zeros], axis=0)
    for k in range(o_ref.shape[1]):
        block = x[:, TILE * k : TILE * k + TILE]
        for i in range(o_ref.shape[0]):
            o_ref[i, k] = block


def embed_kernel(h_ref, a_ref, b_ref, c_ref, d_ref, o_ref, acc_ref):
    step = pl.program_id(0)

    @pl.when(step == 0)
    def _():
        acc_ref[...] = jnp.zeros_like(acc_ref)

    w = jnp.concatenate([a_ref[...], b_ref[...], c_ref[...], d_ref[...]], axis=1)
    acc_ref[...] += matmul(joined(h_ref), w, 1, 0)

    @pl.when(step == pl.num_programs(0) - 1)
    def _():
        o_ref[...] = acc_ref[...].astype(o_ref.dtype)


def center_kernel(rows, samples, own_ref, sib_ref, far_ref, far_sib_ref, c_ref, f_ref, g_ref):
    quarter = own_ref.shape[0]
    blocks = [
        own_ref[...],
        reordered(sib_ref[...], (1, 0, 3, 2)),
        reordered(far_ref[...], (2, 3, 0, 1)),
        reordered(far_sib_ref[...], (3, 2, 1, 0)),
    ]
    wide = [block.astype(jnp.float32) for block in blocks]
    total = wide[0] + wide[1] + wide[2] + wide[3]
    mean = jnp.sum(total, axis=0, keepdims=True) * (1.0 / samples)
    real = lax.broadcasted_iota(jnp.int32, wide[0].shape, 0) % PAD < rows
    squares = jnp.zeros_like(total)
    for i, block in enumerate(wide):
        centered = jnp.where(real, block - mean, 0.0).astype(jnp.bfloat16)
        c_ref[quarter * i : quarter * i + quarter, :] = centered
        centered = centered.astype(jnp.float32)
        squares += centered * centered
    sum_squares = jnp.sum(squares, axis=0, keepdims=True)
    spread_std = jnp.sqrt(sum_squares * (1.0 / (samples - 1)) + 0.0001)
    coef_var = samples / (2.0 * (samples - 1))
    hinge = jax.nn.sigmoid(10.0 * (1.0 - spread_std))
    coef_cov = 0.08 * samples / ((samples - 1) * (samples - 1))
    factor = coef_var * hinge / spread_std + coef_cov * sum_squares
    f_ref[...] = jnp.broadcast_to(factor, f_ref.shape)
    g_ref[...] = matmul(c_ref[:quarter, :], c_ref[...], 1, 1).astype(g_ref.dtype)


def total_kernel(x_ref, o_ref):
    x = x_ref[...].reshape(x_ref.shape[0] // PAD, PAD, x_ref.shape[1])
    total = jnp.sum(x.astype(jnp.float32), axis=0).astype(o_ref.dtype)
    for i in range(o_ref.shape[0] // PAD):
        o_ref[PAD * i : PAD * i + PAD, :] = total


def grad_kernel(rows, samples, m_ref, c_ref, f_ref, e_ref, p_ref, o_ref, *run_refs):
    coef_cov = 0.08 * samples / ((samples - 1) * (samples - 1))
    coupled = matmul(m_ref[...], c_ref[...], 1, 0)
    centered = c_ref[: e_ref.shape[0], :].astype(jnp.float32)
    apart = e_ref[...].astype(jnp.float32) - p_ref[...].astype(jnp.float32)
    grad = apart - f_ref[:1, :] * centered + coef_cov * coupled
    grad = grad.astype(jnp.bfloat16)
    o_ref[...] = grad
    packed = without_padding(grad, rows)
    for i, ref in enumerate(run_refs):
        ref[...] = packed[:, 128 * i : 128 * i + 128]


def hidden_kernel(g_ref, a_ref, b_ref, c_ref, d_ref, o_ref):
    w = jnp.concatenate([a_ref[...], b_ref[...], c_ref[...], d_ref[...]], axis=1)
    out = matmul(g_ref[...], w, 1, 1).astype(o_ref.dtype)
    peers, count, rows, tile = o_ref.shape
    for k in range(count):
        o_ref[:, k] = out[:, tile * k : tile * k + tile].reshape(peers, rows, tile)


def weight_kernel(*refs):
    hs, gs, (o_ref,) = refs[:4], refs[4:8], refs[8:]
    h = jnp.concatenate([ref[...] for ref in hs], axis=0)
    g = jnp.concatenate([ref[...] for ref in gs], axis=0)
    o_ref[...] = matmul(h, g, 0, 0).astype(o_ref.dtype)


def ends_kernel(scale, *refs):
    pairs, (o_ref,) = refs[:-1], refs[-1:]
    at = 0
    for a_ref, b_ref in zip(pairs[::2], pairs[1::2]):
        n = a_ref.shape[0]
        total = a_ref[...].astype(jnp.float32) + b_ref[...].astype(jnp.float32)
        o_ref[at : at + n, :] = total / scale
        at += n


def rows_kernel(x_ref, o_ref):
    total = jnp.sum(x_ref[:, 0].astype(jnp.float32), axis=0)
    o_ref[0] = total[: o_ref.shape[1]]


def copies_of(block, count):
    out = shape((count, block.shape[2] // TILE, PAD, TILE))
    return pl.pallas_call(
        copies_kernel,
        grid=(1,),
        in_specs=[whole(*block.shape)],
        out_specs=whole(*out.shape),
        out_shape=out,
        compiler_params=params(1, FULL),
        cost_estimate=cost(0, 2 * count * block.size),
    )(block)


def embed(plane, weights):
    width, units = weights[0].shape
    rows = plane.size // width
    return pl.pallas_call(
        embed_kernel,
        grid=(width // TILE // 4,),
        in_specs=[columns(plane, 4)]
        + [pl.BlockSpec((4 * TILE, units), lambda k: (k, 0))] * 4,
        out_specs=whole(rows, 4 * units),
        out_shape=shape((rows, 4 * units)),
        scratch_shapes=[pltpu.VMEM((rows, 4 * units), jnp.float32)],
        compiler_params=params(1),
        cost_estimate=cost(8 * rows * width * units, 2 * width * (rows + 4 * units)),
    )(plane, *weights)


def hidden_terms(grad, weights):
    rows = grad.shape[0]
    width, units = weights[0].shape
    out = shape((rows // PAD, width // TILE, PAD, TILE))
    return pl.pallas_call(
        hidden_kernel,
        grid=(width // TILE // 4,),
        in_specs=[whole(*grad.shape)]
        + [pl.BlockSpec((4 * TILE, units), lambda k: (k, 0))] * 4,
        out_specs=columns(out, 4),
        out_shape=out,
        compiler_params=params(1),
        cost_estimate=cost(8 * rows * width * units, 2 * width * (rows + 4 * units)),
    )(grad, *weights)


def hidden_rows(pieces, rows):
    peers, blocks, _, tile = pieces.shape
    return pl.pallas_call(
        rows_kernel,
        grid=(blocks,),
        in_specs=[columns(pieces)],
        out_specs=pl.BlockSpec((1, rows, tile), lambda k: (0, 0, k)),
        out_shape=shape((1, rows, blocks * tile), jnp.float32),
        compiler_params=params(1),
        cost_estimate=cost(pieces.size, 3 * pieces.size),
    )(pieces)


def weight_terms(own, sib, at, far, far_sib, grads):
    rows, width = far.shape
    units = grads[0].shape[1]
    return pl.pallas_call(
        weight_kernel,
        grid=(width // TILE,),
        in_specs=[pl.BlockSpec((rows, TILE), lambda k: (0, k + at // TILE))] * 2
        + [pl.BlockSpec((rows, TILE), lambda k: (0, k))] * 2
        + [whole(*g.shape) for g in grads],
        out_specs=pl.BlockSpec((TILE, units), lambda k: (k, 0)),
        out_shape=shape((width, units)),
        compiler_params=params(1, FULL),
        cost_estimate=cost(8 * rows * width * units, 8 * rows * width),
    )(own, sib, far, far_sib, *grads)


def view_sums(parts, samples):
    arrays = [each for part in parts for each in (part, swap(part, view=1))]
    total = sum(part.shape[0] for part in parts)
    units = parts[0].shape[1]
    return pl.pallas_call(
        functools.partial(ends_kernel, math.sqrt(2.0 * samples)),
        grid=(1,),
        in_specs=[whole(*each.shape) for each in arrays],
        out_specs=whole(total, units),
        out_shape=shape((total, units), jnp.float32),
        compiler_params=params(1, FULL),
        cost_estimate=cost(total * units, 8 * total * units),
    )(*arrays)


def on_device(hidden, weight):
    rows = hidden.shape[1]
    width = hidden.shape[2]
    samples = rows * DP
    units = weight.shape[1]
    peers = YS * XS
    quarter = peers * PAD

    w_far = swap(weight, view=1, z=1)
    w_sib = swap(weight, c=1)
    w_far_sib = swap(w_far, c=1)
    weights = (weight, w_sib, w_far, w_far_sib)

    plane = exchange(copies_of(hidden, peers), "yx")
    plane, w_far_sib = lax.optimization_barrier((plane, w_far_sib))

    mine = embed(plane, weights)
    from_sib = swap(mine, c=1)
    from_far = swap(mine, z=1)
    split = (3 * width // 8, 5 * width // 8)
    from_far, h_own, first, second = lax.optimization_barrier(
        (from_far, *compact(plane, rows, split))
    )
    from_far_sib = swap(from_far, c=1)
    partner = swap(mine, view=1)
    first = swap(first, z=1)

    centered, factor, gram = pl.pallas_call(
        functools.partial(center_kernel, rows, samples),
        grid=(1,),
        in_specs=[whole(quarter, 4 * units)] * 4,
        out_specs=(whole(4 * quarter, 4 * units), whole(8, 4 * units), whole(quarter, 4 * quarter)),
        out_shape=(
            shape((4 * quarter, 4 * units)),
            shape((8, 4 * units), jnp.float32),
            shape((quarter, 4 * quarter)),
        ),
        compiler_params=params(1),
        cost_estimate=cost(8 * 4 * quarter * quarter * units, 16 * quarter * units * 2),
    )(mine, from_sib, from_far, from_far_sib)

    gram, second, partner, late = lax.optimization_barrier((gram, second, partner, h_own))
    h_far = [first, swap(second, z=1)]
    h_sib = swap(late, c=1)
    gram = exchange(gram, "yx")
    gram = pl.pallas_call(
        total_kernel,
        grid=(1,),
        in_specs=[whole(*gram.shape)],
        out_specs=whole(*gram.shape),
        out_shape=shape(gram.shape),
        compiler_params=params(1),
        cost_estimate=cost(gram.size, 4 * gram.size),
    )(gram)
    gram, h_far[0] = lax.optimization_barrier((gram, h_far[0]))
    gram = exchange(gram, "yx")

    grad, *runs = pl.pallas_call(
        functools.partial(grad_kernel, rows, samples),
        grid=(1,),
        in_specs=[
            whole(quarter, 4 * quarter),
            whole(4 * quarter, 4 * units),
            whole(8, 4 * units),
            whole(quarter, 4 * units),
            whole(quarter, 4 * units),
        ],
        out_specs=(whole(quarter, 4 * units),)
        + (whole(peers * rows, units),) * 4,
        out_shape=(shape((quarter, 4 * units)),)
        + (shape((peers * rows, units)),) * 4,
        compiler_params=params(1),
        cost_estimate=cost(8 * 4 * quarter * quarter * units, 16 * quarter * units * 2),
    )(gram, centered, factor, mine, partner)
    g_far = swap(runs[2], z=1)
    g_far_sib = swap(runs[3], z=1, c=1)
    g_sib = swap(runs[1], c=1)
    h_part = hidden_terms(grad, weights)
    h_part, h_sib, h_far[1], *grads = lax.optimization_barrier(
        (h_part, h_sib, h_far[1], runs[0], g_sib, g_far, g_far_sib)
    )
    pieces = exchange(h_part, "yx")

    parts = [
        weight_terms(h_own, h_sib, at, far, swap(far, c=1), grads)
        for at, far in zip((0, split[0]), h_far)
    ]
    grad_weight, pieces = lax.optimization_barrier((view_sums(parts, samples), pieces))
    grad_rows = hidden_rows(pieces, rows)
    return (grad_rows, grad_weight)


def solution(mesh):
    return jax.shard_map(
        on_device,
        mesh=mesh,
        in_specs=(P("view", "dp", None), P(None, "dp")),
        out_specs=(P("view", "dp", None), P(None, "dp")),
        check_vma=False,
    )
```

```python
import functools
import math

import jax
import jax.numpy as jnp
from jax import lax
from jax.experimental import pallas as pl
from jax.experimental.pallas import tpu as pltpu
from jax.sharding import PartitionSpec as P

YS, ZS, XS, CS = 4, 2, 4, 2
DP = YS * ZS * XS * CS
PAD = 16
SMEM = pl.BlockSpec(memory_space=pltpu.SMEM)
TILE = 512
VMEM = 24 * 1024 * 1024


def place(d):
    return (d // (ZS * XS * CS), d // (XS * CS) % ZS, d // CS % XS, d % CS)


def index(y, z, x, c):
    return ((y * ZS + z) * XS + x) * CS + c


def groups(axes):
    found = {}
    for d in range(DP):
        key = tuple(p for p, name in zip(place(d), "yzxc") if name not in axes)
        found.setdefault(key, []).append(d)
    return list(found.values())


def swap(block, view=0, z=0, c=0):
    route = []
    for v in range(2):
        for d in range(DP):
            y, zd, x, cd = place(d)
            route.append((v * DP + d, (v ^ view) * DP + index(y, zd ^ z, x, cd ^ c)))
    return lax.ppermute(block, ("view", "dp"), route)


def exchange(blocks, axes):
    return lax.all_to_all(blocks, "dp", 0, 0, tiled=True, axis_index_groups=groups(axes))


def matmul(a, b, a_dim, b_dim):
    return lax.dot_general(
        a, b, (((a_dim,), (b_dim,)), ((), ())), preferred_element_type=jnp.float32
    )


def rounded(values):
    return lax.optimization_barrier(values.astype(jnp.bfloat16))


def reordered(block, order):
    return jnp.concatenate([block[:, 128 * i : 128 * i + 128] for i in order], axis=1)


def shape(dims, dtype=jnp.bfloat16):
    return jax.ShapeDtypeStruct(dims, dtype)


def params(steps):
    return pltpu.CompilerParams(
        vmem_limit_bytes=VMEM, dimension_semantics=("arbitrary",) * steps
    )


def cost(flops, size):
    return pl.CostEstimate(flops=flops, bytes_accessed=size, transcendentals=0)


def without_padding(x, rows):
    n = x.shape[0] // PAD * rows
    out = lax.broadcasted_iota(jnp.int32, (n, x.shape[0]), 0)
    source = lax.broadcasted_iota(jnp.int32, (n, x.shape[0]), 1)
    pick = out + out // rows * (PAD - rows) == source
    return matmul(jnp.where(pick, 1.0, 0.0).astype(x.dtype), x, 1, 0).astype(x.dtype)


def whole(*dims):
    return pl.BlockSpec(dims, lambda *_: (0,) * len(dims))


def columns(array_or_shape, count=1):
    peers, _, rows, tile = array_or_shape.shape
    return pl.BlockSpec((peers, count, rows, tile), lambda k: (0, k, 0, 0))


def joined(ref):
    n = ref.shape[0] * ref.shape[2]
    blocks = [ref[:, k].reshape(n, ref.shape[3]) for k in range(ref.shape[1])]
    return blocks[0] if len(blocks) == 1 else jnp.concatenate(blocks, axis=1)


def compact_kernel(rows, x_ref, *o_refs):
    at = 0
    for ref in o_refs:
        blocks = ref.shape[1] // TILE
        ref[...] = without_padding(joined(x_ref.at[:, at : at + blocks]), rows)
        at += blocks


def compact(plane, rows, widths):
    peers = plane.shape[0]
    out = tuple(shape((peers * rows, width)) for width in widths)
    return pl.pallas_call(
        functools.partial(compact_kernel, rows),
        grid=(1,),
        in_specs=[whole(*plane.shape)],
        out_specs=tuple(whole(*each.shape) for each in out),
        out_shape=out,
        compiler_params=params(1),
        cost_estimate=cost(4 * plane.size, 4 * plane.size),
    )(plane)


def copies_kernel(x_ref, o_ref):
    x = x_ref[0]
    zeros = jnp.zeros((PAD - x.shape[0], x.shape[1]), x.dtype)
    x = jnp.concatenate([x, zeros], axis=0)
    for k in range(o_ref.shape[1]):
        block = x[:, TILE * k : TILE * k + TILE]
        for i in range(o_ref.shape[0]):
            o_ref[i, k] = block


def embed_kernel(h_ref, a_ref, b_ref, c_ref, d_ref, o_ref, acc_ref):
    step = pl.program_id(0)

    @pl.when(step == 0)
    def _():
        acc_ref[...] = jnp.zeros_like(acc_ref)

    w = jnp.concatenate([a_ref[...], b_ref[...], c_ref[...], d_ref[...]], axis=1)
    acc_ref[...] += matmul(joined(h_ref), w, 1, 0)

    @pl.when(step == pl.num_programs(0) - 1)
    def _():
        o_ref[...] = acc_ref[...].astype(o_ref.dtype)


def center_kernel(rows, samples, own_ref, sib_ref, far_ref, far_sib_ref, c_ref, f_ref, g_ref):
    quarter = own_ref.shape[0]
    blocks = [
        own_ref[...],
        reordered(sib_ref[...], (1, 0, 3, 2)),
        reordered(far_ref[...], (2, 3, 0, 1)),
        reordered(far_sib_ref[...], (3, 2, 1, 0)),
    ]
    wide = [block.astype(jnp.float32) for block in blocks]
    total = wide[0] + wide[1] + wide[2] + wide[3]
    mean = jnp.sum(total, axis=0, keepdims=True) * (1.0 / samples)
    real = lax.broadcasted_iota(jnp.int32, wide[0].shape, 0) % PAD < rows
    squares = jnp.zeros_like(total)
    for i, block in enumerate(wide):
        centered = jnp.where(real, block - mean, 0.0).astype(jnp.bfloat16)
        c_ref[quarter * i : quarter * i + quarter, :] = centered
        centered = centered.astype(jnp.float32)
        squares += centered * centered
    sum_squares = jnp.sum(squares, axis=0, keepdims=True)
    spread_std = jnp.sqrt(sum_squares * (1.0 / (samples - 1)) + 0.0001)
    coef_var = samples / (2.0 * (samples - 1))
    hinge = jax.nn.sigmoid(10.0 * (1.0 - spread_std))
    coef_cov = 0.08 * samples / ((samples - 1) * (samples - 1))
    factor = coef_var * hinge / spread_std + coef_cov * sum_squares
    f_ref[...] = jnp.broadcast_to(factor, f_ref.shape)
    g_ref[...] = matmul(c_ref[:quarter, :], c_ref[...], 1, 1).astype(g_ref.dtype)


def total_kernel(x_ref, o_ref):
    x = x_ref[...].reshape(x_ref.shape[0] // PAD, PAD, x_ref.shape[1])
    total = jnp.sum(x.astype(jnp.float32), axis=0).astype(o_ref.dtype)
    for i in range(o_ref.shape[0] // PAD):
        o_ref[PAD * i : PAD * i + PAD, :] = total


def grad_kernel(rows, samples, me_ref, m_ref, c_ref, f_ref, e_ref, p_ref, o_ref, *run_refs):
    coef_cov = 0.08 * samples / ((samples - 1) * (samples - 1))
    coupled = matmul(m_ref[...], c_ref[...], 1, 0)
    centered = c_ref[: e_ref.shape[0], :].astype(jnp.float32)
    apart = e_ref[...].astype(jnp.float32) - p_ref[...].astype(jnp.float32)
    grad = apart - f_ref[:1, :] * centered + coef_cov * coupled
    grad = grad.astype(jnp.bfloat16)
    o_ref[...] = grad
    packed = without_padding(grad, rows)
    for i in range(4):
        run_refs[0][me_ref[0] ^ i] = packed[:, 128 * i : 128 * i + 128]


def hidden_kernel(g_ref, a_ref, b_ref, c_ref, d_ref, o_ref):
    w = jnp.concatenate([a_ref[...], b_ref[...], c_ref[...], d_ref[...]], axis=1)
    out = matmul(g_ref[...], w, 1, 1).astype(o_ref.dtype)
    peers, count, rows, tile = o_ref.shape
    for k in range(count):
        o_ref[:, k] = out[:, tile * k : tile * k + tile].reshape(peers, rows, tile)


def weight_kernel(me_ref, *refs):
    hs, (g_ref, o_ref) = refs[:4], refs[4:]
    h = jnp.concatenate([ref[...] for ref in hs], axis=0)
    g = jnp.concatenate([g_ref[me_ref[0] ^ i] for i in range(4)], axis=0)
    o_ref[...] = matmul(h, g, 0, 0).astype(o_ref.dtype)


def ends_kernel(scale, *refs):
    pairs, (o_ref,) = refs[:-1], refs[-1:]
    at = 0
    for a_ref, b_ref in zip(pairs[::2], pairs[1::2]):
        n = a_ref.shape[0]
        total = a_ref[...].astype(jnp.float32) + b_ref[...].astype(jnp.float32)
        o_ref[at : at + n, :] = total / scale
        at += n


def rows_kernel(x_ref, o_ref):
    total = jnp.sum(x_ref[:, 0].astype(jnp.float32), axis=0)
    o_ref[0] = total[: o_ref.shape[1]]


def copies_of(block, count):
    out = shape((count, block.shape[2] // TILE, PAD, TILE))
    return pl.pallas_call(
        copies_kernel,
        grid=(1,),
        in_specs=[whole(*block.shape)],
        out_specs=whole(*out.shape),
        out_shape=out,
        compiler_params=params(1),
        cost_estimate=cost(0, 2 * count * block.size),
    )(block)


def embed(plane, weights):
    width, units = weights[0].shape
    rows = plane.size // width
    return pl.pallas_call(
        embed_kernel,
        grid=(width // TILE // 4,),
        in_specs=[columns(plane, 4)]
        + [pl.BlockSpec((4 * TILE, units), lambda k: (k, 0))] * 4,
        out_specs=whole(rows, 4 * units),
        out_shape=shape((rows, 4 * units)),
        scratch_shapes=[pltpu.VMEM((rows, 4 * units), jnp.float32)],
        compiler_params=params(1),
        cost_estimate=cost(8 * rows * width * units, 2 * width * (rows + 4 * units)),
    )(plane, *weights)


def hidden_terms(grad, weights):
    rows = grad.shape[0]
    width, units = weights[0].shape
    out = shape((rows // PAD, width // TILE, PAD, TILE))
    return pl.pallas_call(
        hidden_kernel,
        grid=(width // TILE // 4,),
        in_specs=[whole(*grad.shape)]
        + [pl.BlockSpec((4 * TILE, units), lambda k: (k, 0))] * 4,
        out_specs=columns(out, 4),
        out_shape=out,
        compiler_params=params(1),
        cost_estimate=cost(8 * rows * width * units, 2 * width * (rows + 4 * units)),
    )(grad, *weights)


def hidden_rows(pieces, rows):
    peers, blocks, _, tile = pieces.shape
    return pl.pallas_call(
        rows_kernel,
        grid=(blocks,),
        in_specs=[columns(pieces)],
        out_specs=pl.BlockSpec((1, rows, tile), lambda k: (0, 0, k)),
        out_shape=shape((1, rows, blocks * tile), jnp.float32),
        compiler_params=params(1),
        cost_estimate=cost(pieces.size, 3 * pieces.size),
    )(pieces)


def weight_terms(me, parts, runs):
    rows, width = parts[0].shape
    units = runs.shape[2]
    return pl.pallas_call(
        weight_kernel,
        grid=(width // TILE,),
        in_specs=[SMEM]
        + [pl.BlockSpec((rows, TILE), lambda k: (0, k))] * 4
        + [whole(*runs.shape)],
        out_specs=pl.BlockSpec((TILE, units), lambda k: (k, 0)),
        out_shape=shape((width, units)),
        compiler_params=params(1),
        cost_estimate=cost(8 * rows * width * units, 8 * rows * width),
    )(me, *parts, runs)


def view_sums(parts, samples):
    arrays = [each for part in parts for each in (part, swap(part, view=1))]
    total = sum(part.shape[0] for part in parts)
    units = parts[0].shape[1]
    return pl.pallas_call(
        functools.partial(ends_kernel, math.sqrt(2.0 * samples)),
        grid=(1,),
        in_specs=[whole(*each.shape) for each in arrays],
        out_specs=whole(total, units),
        out_shape=shape((total, units), jnp.float32),
        compiler_params=params(1),
        cost_estimate=cost(total * units, 8 * total * units),
    )(*arrays)


def on_device(hidden, weight):
    rows = hidden.shape[1]
    width = hidden.shape[2]
    samples = rows * DP
    units = weight.shape[1]
    peers = YS * XS
    quarter = peers * PAD

    w_far = swap(weight, view=1, z=1)
    w_sib = swap(weight, c=1)
    w_far_sib = swap(w_far, c=1)
    weights = (weight, w_sib, w_far, w_far_sib)

    plane = exchange(copies_of(hidden, peers), "yx")
    plane, w_far_sib = lax.optimization_barrier((plane, w_far_sib))

    mine = embed(plane, weights)
    from_sib = swap(mine, c=1)
    from_far = swap(mine, z=1)
    split = (3 * width // 8, 5 * width // 8)
    from_far, *h_own = lax.optimization_barrier((from_far, *compact(plane, rows, split)))
    from_far_sib = swap(from_far, c=1)
    partner = swap(mine, view=1)
    first, _ = lax.optimization_barrier((h_own[0], from_far))
    second, partner = lax.optimization_barrier((h_own[1], partner))
    h_far = [swap(first, z=1), swap(second, z=1)]

    centered, factor, gram = pl.pallas_call(
        functools.partial(center_kernel, rows, samples),
        grid=(1,),
        in_specs=[whole(quarter, 4 * units)] * 4,
        out_specs=(whole(4 * quarter, 4 * units), whole(8, 4 * units), whole(quarter, 4 * quarter)),
        out_shape=(
            shape((4 * quarter, 4 * units)),
            shape((8, 4 * units), jnp.float32),
            shape((quarter, 4 * quarter)),
        ),
        compiler_params=params(1),
        cost_estimate=cost(8 * 4 * quarter * quarter * units, 16 * quarter * units * 2),
    )(mine, from_sib, from_far, from_far_sib)

    gram = exchange(gram, "yx")
    gram = pl.pallas_call(
        total_kernel,
        grid=(1,),
        in_specs=[whole(*gram.shape)],
        out_specs=whole(*gram.shape),
        out_shape=shape(gram.shape),
        compiler_params=params(1),
        cost_estimate=cost(gram.size, 4 * gram.size),
    )(gram)
    gram, h_far[0], *late = lax.optimization_barrier((gram, h_far[0], *h_own))
    h_sib = [swap(block, c=1) for block in late]
    gram = exchange(gram, "yx")

    d = lax.axis_index("dp")
    me = (d // (XS * CS) % ZS * CS + d % CS).astype(jnp.int32).reshape(1)
    grad, runs = pl.pallas_call(
        functools.partial(grad_kernel, rows, samples),
        grid=(1,),
        in_specs=[
            SMEM,
            whole(quarter, 4 * quarter),
            whole(4 * quarter, 4 * units),
            whole(8, 4 * units),
            whole(quarter, 4 * units),
            whole(quarter, 4 * units),
        ],
        out_specs=(whole(quarter, 4 * units),)
        + (whole(4, peers * rows, units),),
        out_shape=(shape((quarter, 4 * units)),)
        + (shape((4, peers * rows, units)),),
        compiler_params=params(1),
        cost_estimate=cost(8 * 4 * quarter * quarter * units, 16 * quarter * units * 2),
    )(me, gram, centered, factor, mine, partner)
    runs = exchange(runs, "zc")

    h_part = hidden_terms(grad, weights)
    h_part, h_far[1], runs = lax.optimization_barrier((h_part, h_far[1], runs))
    pieces = exchange(h_part, "yx")

    parts = [
        weight_terms(me, (own, sib, far, swap(far, c=1)), runs)
        for own, sib, far in zip(h_own, h_sib, h_far)
    ]
    grad_weight, pieces = lax.optimization_barrier((view_sums(parts, samples), pieces))
    grad_rows = hidden_rows(pieces, rows)
    return (grad_rows, grad_weight)


def solution(mesh):
    return jax.shard_map(
        on_device,
        mesh=mesh,
        in_specs=(P("view", "dp", None), P(None, "dp")),
        out_specs=(P("view", "dp", None), P(None, "dp")),
        check_vma=False,
    )
```

```python
import functools
import math

import jax
import jax.numpy as jnp
from jax import lax
from jax.experimental import pallas as pl
from jax.experimental.pallas import tpu as pltpu
from jax.sharding import PartitionSpec as P

YS, ZS, XS, CS = 4, 2, 4, 2
DP = YS * ZS * XS * CS
PAD = 16
SMEM = pl.BlockSpec(memory_space=pltpu.SMEM)
TILE = 512
VMEM = 24 * 1024 * 1024


def place(d):
    return (d // (ZS * XS * CS), d // (XS * CS) % ZS, d // CS % XS, d % CS)


def index(y, z, x, c):
    return ((y * ZS + z) * XS + x) * CS + c


def groups(axes):
    found = {}
    for d in range(DP):
        key = tuple(p for p, name in zip(place(d), "yzxc") if name not in axes)
        found.setdefault(key, []).append(d)
    return list(found.values())


def swap(block, view=0, z=0, c=0):
    route = []
    for v in range(2):
        for d in range(DP):
            y, zd, x, cd = place(d)
            route.append((v * DP + d, (v ^ view) * DP + index(y, zd ^ z, x, cd ^ c)))
    return lax.ppermute(block, ("view", "dp"), route)


def exchange(blocks, axes):
    return lax.all_to_all(blocks, "dp", 0, 0, tiled=True, axis_index_groups=groups(axes))


def matmul(a, b, a_dim, b_dim):
    return lax.dot_general(
        a, b, (((a_dim,), (b_dim,)), ((), ())), preferred_element_type=jnp.float32
    )


def rounded(values):
    return lax.optimization_barrier(values.astype(jnp.bfloat16))


def reordered(block, order):
    return jnp.concatenate([block[:, 128 * i : 128 * i + 128] for i in order], axis=1)


def shape(dims, dtype=jnp.bfloat16):
    return jax.ShapeDtypeStruct(dims, dtype)


def params(steps):
    return pltpu.CompilerParams(
        vmem_limit_bytes=VMEM, dimension_semantics=("arbitrary",) * steps
    )


def cost(flops, size):
    return pl.CostEstimate(flops=flops, bytes_accessed=size, transcendentals=0)


def without_padding(x, rows):
    n = x.shape[0] // PAD * rows
    out = lax.broadcasted_iota(jnp.int32, (n, x.shape[0]), 0)
    source = lax.broadcasted_iota(jnp.int32, (n, x.shape[0]), 1)
    pick = out + out // rows * (PAD - rows) == source
    return matmul(jnp.where(pick, 1.0, 0.0).astype(x.dtype), x, 1, 0).astype(x.dtype)


def whole(*dims):
    return pl.BlockSpec(dims, lambda *_: (0,) * len(dims))


def columns(array_or_shape, count=1):
    peers, _, rows, tile = array_or_shape.shape
    return pl.BlockSpec((peers, count, rows, tile), lambda k: (0, k, 0, 0))


def joined(ref):
    n = ref.shape[0] * ref.shape[2]
    blocks = [ref[:, k].reshape(n, ref.shape[3]) for k in range(ref.shape[1])]
    return blocks[0] if len(blocks) == 1 else jnp.concatenate(blocks, axis=1)


def compact_kernel(rows, x_ref, *o_refs):
    at = 0
    for ref in o_refs:
        blocks = ref.shape[1] // TILE
        ref[...] = without_padding(joined(x_ref.at[:, at : at + blocks]), rows)
        at += blocks


def compact(plane, rows, widths):
    peers = plane.shape[0]
    out = tuple(shape((peers * rows, width)) for width in widths)
    return pl.pallas_call(
        functools.partial(compact_kernel, rows),
        grid=(1,),
        in_specs=[whole(*plane.shape)],
        out_specs=tuple(whole(*each.shape) for each in out),
        out_shape=out,
        compiler_params=params(1),
        cost_estimate=cost(4 * plane.size, 4 * plane.size),
    )(plane)


def copies_kernel(x_ref, o_ref):
    x = x_ref[0]
    zeros = jnp.zeros((PAD - x.shape[0], x.shape[1]), x.dtype)
    x = jnp.concatenate([x, zeros], axis=0)
    for k in range(o_ref.shape[1]):
        block = x[:, TILE * k : TILE * k + TILE]
        for i in range(o_ref.shape[0]):
            o_ref[i, k] = block


def embed_kernel(h_ref, a_ref, b_ref, c_ref, d_ref, o_ref, acc_ref):
    step = pl.program_id(0)

    @pl.when(step == 0)
    def _():
        acc_ref[...] = jnp.zeros_like(acc_ref)

    w = jnp.concatenate([a_ref[...], b_ref[...], c_ref[...], d_ref[...]], axis=1)
    acc_ref[...] += matmul(joined(h_ref), w, 1, 0)

    @pl.when(step == pl.num_programs(0) - 1)
    def _():
        o_ref[...] = acc_ref[...].astype(o_ref.dtype)


def center_kernel(rows, samples, own_ref, sib_ref, far_ref, far_sib_ref, c_ref, f_ref, g_ref):
    quarter = own_ref.shape[0]
    blocks = [
        own_ref[...],
        reordered(sib_ref[...], (1, 0, 3, 2)),
        reordered(far_ref[...], (2, 3, 0, 1)),
        reordered(far_sib_ref[...], (3, 2, 1, 0)),
    ]
    wide = [block.astype(jnp.float32) for block in blocks]
    total = wide[0] + wide[1] + wide[2] + wide[3]
    mean = jnp.sum(total, axis=0, keepdims=True) * (1.0 / samples)
    real = lax.broadcasted_iota(jnp.int32, wide[0].shape, 0) % PAD < rows
    squares = jnp.zeros_like(total)
    for i, block in enumerate(wide):
        centered = jnp.where(real, block - mean, 0.0).astype(jnp.bfloat16)
        c_ref[quarter * i : quarter * i + quarter, :] = centered
        centered = centered.astype(jnp.float32)
        squares += centered * centered
    sum_squares = jnp.sum(squares, axis=0, keepdims=True)
    spread_std = jnp.sqrt(sum_squares * (1.0 / (samples - 1)) + 0.0001)
    coef_var = samples / (2.0 * (samples - 1))
    hinge = jax.nn.sigmoid(10.0 * (1.0 - spread_std))
    coef_cov = 0.08 * samples / ((samples - 1) * (samples - 1))
    factor = coef_var * hinge / spread_std + coef_cov * sum_squares
    f_ref[...] = jnp.broadcast_to(factor, f_ref.shape)
    g_ref[...] = matmul(c_ref[:quarter, :], c_ref[...], 1, 1).astype(g_ref.dtype)


def total_kernel(x_ref, o_ref):
    x = x_ref[...].reshape(x_ref.shape[0] // PAD, PAD, x_ref.shape[1])
    total = jnp.sum(x.astype(jnp.float32), axis=0).astype(o_ref.dtype)
    for i in range(o_ref.shape[0] // PAD):
        o_ref[PAD * i : PAD * i + PAD, :] = total


def grad_kernel(rows, samples, me_ref, m_ref, c_ref, f_ref, e_ref, p_ref, o_ref, *run_refs):
    coef_cov = 0.08 * samples / ((samples - 1) * (samples - 1))
    coupled = matmul(m_ref[...], c_ref[...], 1, 0)
    centered = c_ref[: e_ref.shape[0], :].astype(jnp.float32)
    apart = e_ref[...].astype(jnp.float32) - p_ref[...].astype(jnp.float32)
    grad = apart - f_ref[:1, :] * centered + coef_cov * coupled
    grad = grad.astype(jnp.bfloat16)
    o_ref[...] = grad
    packed = without_padding(grad, rows)
    for i in range(4):
        run_refs[0][me_ref[0] ^ i] = packed[:, 128 * i : 128 * i + 128]


def hidden_kernel(g_ref, a_ref, b_ref, c_ref, d_ref, o_ref):
    w = jnp.concatenate([a_ref[...], b_ref[...], c_ref[...], d_ref[...]], axis=1)
    out = matmul(g_ref[...], w, 1, 1).astype(o_ref.dtype)
    peers, count, rows, tile = o_ref.shape
    for k in range(count):
        o_ref[:, k] = out[:, tile * k : tile * k + tile].reshape(peers, rows, tile)


def weight_kernel(me_ref, *refs):
    hs, (g_ref, o_ref) = refs[:4], refs[4:]
    h = jnp.concatenate([ref[...] for ref in hs], axis=0)
    g = jnp.concatenate([g_ref[me_ref[0] ^ i] for i in range(4)], axis=0)
    o_ref[...] = matmul(h, g, 0, 0).astype(o_ref.dtype)


def ends_kernel(scale, *refs):
    pairs, (o_ref,) = refs[:-1], refs[-1:]
    at = 0
    for a_ref, b_ref in zip(pairs[::2], pairs[1::2]):
        n = a_ref.shape[0]
        total = a_ref[...].astype(jnp.float32) + b_ref[...].astype(jnp.float32)
        o_ref[at : at + n, :] = total / scale
        at += n


def rows_kernel(x_ref, o_ref):
    total = jnp.sum(x_ref[:, 0].astype(jnp.float32), axis=0)
    o_ref[0] = total[: o_ref.shape[1]]


def copies_of(block, count):
    out = shape((count, block.shape[2] // TILE, PAD, TILE))
    return pl.pallas_call(
        copies_kernel,
        grid=(1,),
        in_specs=[whole(*block.shape)],
        out_specs=whole(*out.shape),
        out_shape=out,
        compiler_params=params(1),
        cost_estimate=cost(0, 2 * count * block.size),
    )(block)


def embed(plane, weights):
    width, units = weights[0].shape
    rows = plane.size // width
    return pl.pallas_call(
        embed_kernel,
        grid=(width // TILE // 4,),
        in_specs=[columns(plane, 4)]
        + [pl.BlockSpec((4 * TILE, units), lambda k: (k, 0))] * 4,
        out_specs=whole(rows, 4 * units),
        out_shape=shape((rows, 4 * units)),
        scratch_shapes=[pltpu.VMEM((rows, 4 * units), jnp.float32)],
        compiler_params=params(1),
        cost_estimate=cost(8 * rows * width * units, 2 * width * (rows + 4 * units)),
    )(plane, *weights)


def hidden_terms(grad, weights):
    rows = grad.shape[0]
    width, units = weights[0].shape
    out = shape((rows // PAD, width // TILE, PAD, TILE))
    return pl.pallas_call(
        hidden_kernel,
        grid=(width // TILE // 4,),
        in_specs=[whole(*grad.shape)]
        + [pl.BlockSpec((4 * TILE, units), lambda k: (k, 0))] * 4,
        out_specs=columns(out, 4),
        out_shape=out,
        compiler_params=params(1),
        cost_estimate=cost(8 * rows * width * units, 2 * width * (rows + 4 * units)),
    )(grad, *weights)


def hidden_rows(pieces, rows):
    peers, blocks, _, tile = pieces.shape
    return pl.pallas_call(
        rows_kernel,
        grid=(blocks,),
        in_specs=[columns(pieces)],
        out_specs=pl.BlockSpec((1, rows, tile), lambda k: (0, 0, k)),
        out_shape=shape((1, rows, blocks * tile), jnp.float32),
        compiler_params=params(1),
        cost_estimate=cost(pieces.size, 3 * pieces.size),
    )(pieces)


def weight_terms(me, parts, runs):
    rows, width = parts[0].shape
    units = runs.shape[2]
    return pl.pallas_call(
        weight_kernel,
        grid=(width // TILE,),
        in_specs=[SMEM]
        + [pl.BlockSpec((rows, TILE), lambda k: (0, k))] * 4
        + [whole(*runs.shape)],
        out_specs=pl.BlockSpec((TILE, units), lambda k: (k, 0)),
        out_shape=shape((width, units)),
        compiler_params=params(1),
        cost_estimate=cost(8 * rows * width * units, 8 * rows * width),
    )(me, *parts, runs)


def view_sums(parts, samples):
    arrays = [each for part in parts for each in (part, swap(part, view=1))]
    total = sum(part.shape[0] for part in parts)
    units = parts[0].shape[1]
    return pl.pallas_call(
        functools.partial(ends_kernel, math.sqrt(2.0 * samples)),
        grid=(1,),
        in_specs=[whole(*each.shape) for each in arrays],
        out_specs=whole(total, units),
        out_shape=shape((total, units), jnp.float32),
        compiler_params=params(1),
        cost_estimate=cost(total * units, 8 * total * units),
    )(*arrays)


def on_device(hidden, weight):
    rows = hidden.shape[1]
    width = hidden.shape[2]
    samples = rows * DP
    units = weight.shape[1]
    peers = YS * XS
    quarter = peers * PAD

    w_far = swap(weight, view=1, z=1)
    w_sib = swap(weight, c=1)
    w_far_sib = swap(w_far, c=1)
    weights = (weight, w_sib, w_far, w_far_sib)

    plane = exchange(copies_of(hidden, peers), "yx")
    plane, w_far_sib = lax.optimization_barrier((plane, w_far_sib))

    mine = embed(plane, weights)
    from_sib = swap(mine, c=1)
    from_far = swap(mine, z=1)
    split = (width // 4, 3 * width // 4)
    from_far, *h_own = lax.optimization_barrier((from_far, *compact(plane, rows, split)))
    from_far_sib = swap(from_far, c=1)
    partner = swap(mine, view=1)
    first, _ = lax.optimization_barrier((h_own[0], from_far))
    second, partner = lax.optimization_barrier((h_own[1], partner))
    h_far = [swap(first, z=1), swap(second, z=1)]

    centered, factor, gram = pl.pallas_call(
        functools.partial(center_kernel, rows, samples),
        grid=(1,),
        in_specs=[whole(quarter, 4 * units)] * 4,
        out_specs=(whole(4 * quarter, 4 * units), whole(8, 4 * units), whole(quarter, 4 * quarter)),
        out_shape=(
            shape((4 * quarter, 4 * units)),
            shape((8, 4 * units), jnp.float32),
            shape((quarter, 4 * quarter)),
        ),
        compiler_params=params(1),
        cost_estimate=cost(8 * 4 * quarter * quarter * units, 16 * quarter * units * 2),
    )(mine, from_sib, from_far, from_far_sib)

    gram = exchange(gram, "yx")
    gram = pl.pallas_call(
        total_kernel,
        grid=(1,),
        in_specs=[whole(*gram.shape)],
        out_specs=whole(*gram.shape),
        out_shape=shape(gram.shape),
        compiler_params=params(1),
        cost_estimate=cost(gram.size, 4 * gram.size),
    )(gram)
    gram = exchange(gram, "yx")

    d = lax.axis_index("dp")
    me = (d // (XS * CS) % ZS * CS + d % CS).astype(jnp.int32).reshape(1)
    grad, runs = pl.pallas_call(
        functools.partial(grad_kernel, rows, samples),
        grid=(1,),
        in_specs=[
            SMEM,
            whole(quarter, 4 * quarter),
            whole(4 * quarter, 4 * units),
            whole(8, 4 * units),
            whole(quarter, 4 * units),
            whole(quarter, 4 * units),
        ],
        out_specs=(whole(quarter, 4 * units),)
        + (whole(4, peers * rows, units),),
        out_shape=(shape((quarter, 4 * units)),)
        + (shape((4, peers * rows, units)),),
        compiler_params=params(1),
        cost_estimate=cost(8 * 4 * quarter * quarter * units, 16 * quarter * units * 2),
    )(me, gram, centered, factor, mine, partner)
    runs = exchange(runs, "zc")

    h_part = hidden_terms(grad, weights)
    h_part, runs, *h_far = lax.optimization_barrier((h_part, runs, *h_far))
    h_sib = [swap(block, c=1) for block in h_own]
    pieces = exchange(h_part, "yx")

    parts = [
        weight_terms(me, (own, sib, far, swap(far, c=1)), runs)
        for own, sib, far in zip(h_own, h_sib, h_far)
    ]
    grad_weight, pieces = lax.optimization_barrier((view_sums(parts, samples), pieces))
    grad_rows = hidden_rows(pieces, rows)
    return (grad_rows, grad_weight)


def solution(mesh):
    return jax.shard_map(
        on_device,
        mesh=mesh,
        in_specs=(P("view", "dp", None), P(None, "dp")),
        out_specs=(P("view", "dp", None), P(None, "dp")),
        check_vma=False,
    )
```
